512 devices in a mesh: row: 32 (over y_lo, z, core), col: 16 (over y_hi, x).
Axes of the slice: x: 4, y: 8 (y_hi: 4, y_lo: 2; y = y_hi * 2 + y_lo), z: 8, core: 2. Of those that a mesh axis runs over, the one named last changes fastest.
Arguments:
- tokens: bfloat16 [256, 512, 256], P('row', 'col'), may hold values from -6 to 6
- fine_proj: bfloat16 [256, 768], replicated, may hold values from -0.375 to 0.375
- fine_scale: float32 [4], replicated, may hold values from 3 to 12
- coarse_proj: bfloat16 [3, 1024, 1024], P(None, None, 'col'), may hold values from -0.1875 to 0.1875
- coarse_scale: float32 [16], P('col'), may hold values from 12 to 40
- coarse_cot: bfloat16 [32, 64, 1024], P('row', None, 'col'), may hold values from -6 to 6
Outputs:
- coarse_out: float32 [32, 64, 1024], P('row', None, 'col')
- fine_grad: bfloat16 [256, 512, 256], P('row', 'col')
The draws below stay inside these ranges and needn't reach their ends.
All inputs are finite; a program needn't handle non-finite values.
Results may differ from the reference program's by a relative error of at most 0.035.
Values may be sent and summed in bfloat16 or wider, within the bound.
A program may use at most 64 MiB of HBM per device.

```python
import math
from functools import partial
import jax
import jax.numpy as jnp
from jax import lax

DF = 256
HF = 4
DC = 1024
HC = 16
H = 256
W = 512
NCR = 32
NCC = 64


def steps_of(key, shape, shards, low, largest):
    factor_of, own = 1.0, jax.random.fold_in(key, 6)
    for dim, blocks in shards:
        steps = jnp.exp(jax.random.uniform(jax.random.fold_in(own, dim), (blocks,), jnp.float32, low / len(shards), largest / len(shards)))
        factor_of = factor_of * jnp.repeat(steps, shape[dim] // blocks).reshape([-1 if axis == dim else 1 for axis in range(len(shape))])
    return factor_of


def gaussian(own_key, dims, scale, reach, shards=(), dtype=jnp.bfloat16):
    loudness = steps_of(own_key, dims, shards, -0.22, 0.18) if shards else 1.0
    values = jax.random.normal(own_key, dims, jnp.float32) * scale * loudness
    return jnp.minimum(jnp.maximum(values, -reach), reach).astype(dtype)


def setup_inputs(seed: int = 0) -> dict:
    seeds = jax.random.split(jax.random.key(seed), 7)
    return {
        "tokens": gaussian(seeds[0], (H, W, DF), 1.0, 6.0, ((0, 32), (1, 16))),
        "fine_proj": gaussian(seeds[1], (DF, 3 * DF), DF ** -0.5, 0.375),
        "fine_scale": jnp.clip(jnp.exp(jax.random.uniform(seeds[2], (HF,), jnp.float32, math.log(3.0), math.log(12.0))), 3.0, 12.0),
        "coarse_proj": gaussian(seeds[3], (3, DC, DC), DC ** -0.5, 0.1875, ((2, 16),)),
        "coarse_scale": jnp.clip(jnp.exp(math.log(40.0) - 1.2039728 * jax.random.uniform(seeds[4], (HC,), jnp.float32) ** steps_of(seeds[4], (HC,), ((0, 16),), -0.2, 0.2)), 12.0, 40.0),
        "coarse_cot": gaussian(seeds[5], (NCR, NCC, DC), 1.0, 6.0, ((0, 32), (2, 16))),
    }


epsilon = 1e-06

def unit_rows(tensor, scales):
    inverse = lax.rsqrt(lax.optimization_barrier(jnp.sum(tensor * tensor, axis=-1, keepdims=True)) + epsilon)
    return tensor * inverse * scales[:, None]

def rms_norm(field):
    return field * lax.rsqrt(lax.optimization_barrier(jnp.mean(field * field, axis=-1, keepdims=True)) + epsilon)

def merge_cells(field):
    height, breadth, width = field.shape
    grouped = field.reshape(height // 8, 2, 4, breadth // 8, 2, 4, width)
    pooled = lax.optimization_barrier(jnp.mean(grouped, axis=(2, 5)))
    return jnp.transpose(pooled, (0, 2, 1, 3, 4)).reshape(height // 8, breadth // 8, 4 * width)

def spread_cells(gradient, width):
    coarse_rows = gradient.shape[0]
    coarse_columns = gradient.shape[1]
    shaped = jnp.transpose(gradient.reshape(coarse_rows, coarse_columns, 2, 2, width), (0, 2, 1, 3, 4))
    expanded = jnp.broadcast_to(shaped[:, :, None, :, :, None, :] / 16.0, (coarse_rows, 2, 4, coarse_columns, 2, 4, width))
    return expanded.reshape(coarse_rows * 8, coarse_columns * 8, width)

def head_forward(inputs):
    query_head, key_head, value_head = inputs
    scores = jnp.dot(query_head, key_head.T, preferred_element_type=jnp.float32)
    weights = jnp.exp(scores)
    total = lax.optimization_barrier(jnp.sum(weights, axis=1))
    summed = jnp.dot(weights.astype(jnp.bfloat16), value_head, preferred_element_type=jnp.float32)
    return (summed / total[:, None], total)

def head_backward(inputs):
    query_head, key_head, value_head, cot_head, total, delta = inputs
    scores = jnp.dot(query_head, key_head.T, preferred_element_type=jnp.float32)
    shares = jnp.exp(scores) / total[:, None]
    share_grad = jnp.dot(cot_head, value_head.T, preferred_element_type=jnp.float32)
    score_grad = (shares * (share_grad - delta[:, None])).astype(jnp.bfloat16)
    query_grad = jnp.dot(score_grad, key_head, preferred_element_type=jnp.float32)
    key_grad = jnp.dot(score_grad.T, query_head, preferred_element_type=jnp.float32)
    value_grad = jnp.dot(shares.astype(jnp.bfloat16).T, cot_head, preferred_element_type=jnp.float32)
    return (query_grad, key_grad, value_grad)

def reference(tokens, fine_proj, fine_scale, coarse_proj, coarse_scale, coarse_cot):
    height, breadth, width = tokens.shape
    heads = fine_scale.shape[0]
    depth = width // heads
    mixed = jnp.dot(tokens.reshape(-1, width), fine_proj, preferred_element_type=jnp.float32)
    mixed = mixed.reshape(height, breadth, 3 * width)
    raw_query = mixed[..., :width].reshape(height, breadth, heads, depth)
    raw_key = mixed[..., width:2 * width].reshape(height, breadth, heads, depth)
    ones_fine = jnp.ones((heads,), jnp.float32)
    query_half = unit_rows(raw_query, fine_scale).astype(jnp.bfloat16)
    key_half = unit_rows(raw_key, ones_fine).astype(jnp.bfloat16)
    value_half = mixed[..., 2 * width:].astype(jnp.bfloat16).reshape(height, breadth, heads, depth)
    key_pad = jnp.pad(key_half, ((3, 3), (3, 3), (0, 0), (0, 0)))
    value_pad = jnp.pad(value_half, ((3, 3), (3, 3), (0, 0), (0, 0)))
    inside = jnp.pad(jnp.ones((height, breadth), jnp.float32), 3) > 0.5
    query_float = query_half.astype(jnp.float32)

    def window(down_step, across):
        near_key = key_pad[down_step:down_step + height, across:across + breadth].astype(jnp.float32)
        near_value = value_pad[down_step:down_step + height, across:across + breadth].astype(jnp.float32)
        valid = inside[down_step:down_step + height, across:across + breadth]
        scores = lax.optimization_barrier(jnp.sum(query_float * near_key, axis=-1))
        weights = jnp.where(valid[:, :, None], jnp.exp(scores), 0.0)
        return (near_key, near_value, weights)
    total = jnp.zeros((height, breadth, heads), jnp.float32)
    summed = jnp.zeros((height, breadth, heads, depth), jnp.float32)
    for down_step in range(7):
        for across in range(7):
            near_key, near_value, weights = window(down_step, across)
            total = total + weights
            summed = summed + weights.astype(jnp.bfloat16).astype(jnp.float32)[..., None] * near_value
    attend = summed / total[..., None]
    resid = tokens.astype(jnp.float32) + attend.reshape(height, breadth, width)
    merged = merge_cells(resid)
    normed_half = rms_norm(merged).astype(jnp.bfloat16)
    coarse_rows, coarse_columns, coarse_width = merged.shape
    merged_count = coarse_rows * coarse_columns
    cheads = coarse_scale.shape[0]
    cdepth = coarse_width // cheads
    flat_normed = normed_half.reshape(merged_count, coarse_width)
    made = jnp.einsum('td,sde->tse', flat_normed, coarse_proj, preferred_element_type=jnp.float32)
    raw_cquery = made[:, 0].reshape(merged_count, cheads, cdepth)
    raw_ckey = made[:, 1].reshape(merged_count, cheads, cdepth)
    coarse_query = unit_rows(raw_cquery, coarse_scale).astype(jnp.bfloat16)
    coarse_key = unit_rows(raw_ckey, jnp.ones((cheads,), jnp.float32)).astype(jnp.bfloat16)
    coarse_value = made[:, 2].astype(jnp.bfloat16).reshape(merged_count, cheads, cdepth)
    query_heads = jnp.transpose(coarse_query, (1, 0, 2))
    key_heads = jnp.transpose(coarse_key, (1, 0, 2))
    value_heads = jnp.transpose(coarse_value, (1, 0, 2))
    coarse_att, coarse_total = lax.map(head_forward, (query_heads, key_heads, value_heads))
    attention = jnp.transpose(coarse_att, (1, 0, 2)).reshape(merged_count, coarse_width)
    coarse_out = (flat_normed.astype(jnp.float32) + attention).reshape(coarse_rows, coarse_columns, coarse_width)
    cotangent = coarse_cot.reshape(merged_count, coarse_width)
    cot_heads = jnp.transpose(cotangent.reshape(merged_count, cheads, cdepth), (1, 0, 2))
    coarse_delta = lax.optimization_barrier(jnp.sum(cot_heads.astype(jnp.float32) * coarse_att, axis=2))
    grad_cq, grad_ck, grad_cv = lax.map(head_backward, (query_heads, key_heads, value_heads, cot_heads, coarse_total, coarse_delta))
    grad_cq = jnp.transpose(grad_cq, (1, 0, 2))
    grad_ck = jnp.transpose(grad_ck, (1, 0, 2))
    grad_cv = jnp.transpose(grad_cv, (1, 0, 2)).reshape(merged_count, coarse_width)
    _, pull_cquery = jax.vjp(partial(unit_rows, scales=coarse_scale), raw_cquery)
    _, pull_ckey = jax.vjp(partial(unit_rows, scales=jnp.ones((cheads,), jnp.float32)), raw_ckey)
    raw_cq_grad, = pull_cquery(grad_cq)
    raw_ck_grad, = pull_ckey(grad_ck)
    grads_half = jnp.stack([raw_cq_grad.reshape(merged_count, coarse_width), raw_ck_grad.reshape(merged_count, coarse_width), grad_cv], axis=1).astype(jnp.bfloat16)
    grad_normed = jnp.einsum('tse,sde->td', grads_half, coarse_proj, preferred_element_type=jnp.float32) + cotangent.astype(jnp.float32)
    _, pull_norm = jax.vjp(rms_norm, merged)
    grad_merged, = pull_norm(grad_normed.reshape(coarse_rows, coarse_columns, coarse_width))
    grad_fine = spread_cells(grad_merged, width).astype(jnp.bfloat16)
    cot_float = grad_fine.astype(jnp.float32).reshape(height, breadth, heads, depth)
    fine_delta = lax.optimization_barrier(jnp.sum(cot_float * attend, axis=-1))
    grad_query = jnp.zeros((height, breadth, heads, depth), jnp.float32)
    key_back = jnp.zeros((height + 6, breadth + 6, heads, depth), jnp.float32)
    value_back = jnp.zeros((height + 6, breadth + 6, heads, depth), jnp.float32)
    for down_step in range(7):
        for across in range(7):
            near_key, near_value, weights = window(down_step, across)
            shares = weights / total
            share_grad = lax.optimization_barrier(jnp.sum(cot_float * near_value, axis=-1))
            score_grad = (shares * (share_grad - fine_delta)).astype(jnp.bfloat16).astype(jnp.float32)
            grad_query = grad_query + score_grad[..., None] * near_key
            key_back = key_back.at[down_step:down_step + height, across:across + breadth].add(score_grad[..., None] * query_float)
            value_back = value_back.at[down_step:down_step + height, across:across + breadth].add(shares.astype(jnp.bfloat16).astype(jnp.float32)[..., None] * cot_float)
    grad_key = key_back[3:3 + height, 3:3 + breadth]
    grad_value = value_back[3:3 + height, 3:3 + breadth]
    _, pull_query = jax.vjp(partial(unit_rows, scales=fine_scale), raw_query)
    _, pull_key = jax.vjp(partial(unit_rows, scales=ones_fine), raw_key)
    raw_q_grad, = pull_query(grad_query)
    raw_k_grad, = pull_key(grad_key)
    fine_half = jnp.concatenate([raw_q_grad.reshape(-1, width), raw_k_grad.reshape(-1, width), grad_value.reshape(-1, width)], axis=1).astype(jnp.bfloat16)
    back = lax.dot_general(fine_half, fine_proj, (((1,), (1,)), ((), ())), preferred_element_type=jnp.float32)
    fine_grad = (grad_fine.reshape(-1, width).astype(jnp.float32) + back).astype(jnp.bfloat16).reshape(height, breadth, width)
    return (coarse_out, fine_grad)
```

```python
import contextlib

import jax
import jax.numpy as jnp
from jax import lax
from jax.experimental import pallas as pl
from jax.experimental.pallas import tpu as pltpu
from jax.sharding import PartitionSpec as P

F32 = jnp.float32
BF = jnp.bfloat16
I32 = jnp.int32
EPS = 1e-06
MESH = pl.DeviceIdType.MESH

NY, NZ, NCORE = 2, 8, 2
NR, NC = NY * NZ * NCORE, 16
ROWS, COLS, WIDTH, HEADS = 8, 32, 256, 4
TOKENS = ROWS * COLS
HALO = 320
KEYS = 640
OWN = slice(0, 256)
HALF_HALO = (slice(256, 512), slice(384, 640))
CT = 4 * NC
CD = 64
NM = NY * NCORE

DIRS = ((-1, 0), (1, 0), (0, -1), (0, 1), (-1, -1), (-1, 1), (1, -1), (1, 1))
OPPOSITE = (1, 0, 3, 2, 7, 6, 5, 4)
START = (0, 96, 192, 224, 256, 272, 288, 304)
PLACE = (288, 512, 384, 416, 448, 464, 480, 496)
LENGTH = (96, 96, 32, 32, 16, 16, 16, 16)


def mm(a, b):
    return jnp.dot(a, b, preferred_element_type=F32)


def mt(a, b):
    return lax.dot_general(a, b, (((1,), (1,)), ((), ())), preferred_element_type=F32)


def iota(shape, dim):
    return lax.broadcasted_iota(I32, shape, dim)


def onehot(condition):
    return jnp.where(condition, 1.0, 0.0).astype(BF)


def third(m):
    return (m * 11) >> 5


def edge_parts(p):
    side = p < 64
    m = jnp.where(side, p & 31, p & 15)
    down = third(m)
    across = m - 3 * down
    right = jnp.where(side, (p >> 5) & 1, (p >> 4) & 1)
    bottom = jnp.where(side, 0, ((p - 64) >> 5) & 1)
    used = m < jnp.where(side, 24, 9)
    return side, down, across, right, bottom, used


def kernel(
    tok_hbm, fproj_hbm, fscale_hbm, cproj, cscale, cot_hbm,
    out_c, out_f,
    tok, fproj, fscale, cot, kvx, staging, rq_s, rk_s, iq_s, ik_s, qh, qt, pt, psum, fot, fo_s, kt, fproj_t, wxt, wide, cg, mm_s, inv_s,
    eye_s, w_kv, w_qc, select_s,
    kv, qc, st, ce_s, dp_s, cds_s, dkv, dkv_in, dqo, dqo_in, sb, rb, dyt, ds, dk_halo, dv_halo, rh_k, rh_v,
    in_sem, w_sem, halo_ss, halo_rs, cg_ss, cg_rs, kv_ss, kv_rs, qc_ss, qc_rs, st_ss, st_rs,
    dkv_ss, dkv_rs, dqo_ss, dqo_rs, rs_ss, rs_rs, back_ss, back_rs,
):
    row = lax.axis_index("row")
    col = lax.axis_index("col")
    core = row % NCORE
    z = (row // NCORE) % NZ
    y = row // (NCORE * NZ)
    mate = y * NCORE + core
    col_hi = col // 4
    col_lo = col % 4

    def index_of(m, zz):
        return ((m // NCORE) * NZ + zz) * NCORE + m % NCORE

    def neighbour(k):
        return (row + DIRS[k][0] + NR) % NR, (col + DIRS[k][1] + NC) % NC

    z_steps = (4, 3, 5, 2, 6, 1, 7)
    col_steps = sorted(
        ((hi, lo) for hi in range(4) for lo in range(4) if (hi, lo) != (0, 0)),
        key=lambda s: -(2 * min(s[0], 4 - s[0]) + min(s[1], 4 - s[1])),
    )
    z_peers = [(z + d) % NZ for d in z_steps]
    mates = [(mate + d) % NM for d in range(1, NM)]
    col_peers = [((col_hi + hi) % 4) * 4 + (col_lo + lo) % 4 for hi, lo in col_steps]

    open_scope = contextlib.ExitStack()

    def phase(name):
        open_scope.close()
        open_scope.enter_context(jax.named_scope(name))

    barrier = pltpu.get_barrier_semaphore()

    def greet(r, c):
        pl.semaphore_signal(barrier, inc=1, device_id=(r, c), device_id_type=MESH)

    phase("greet")
    for c in col_peers[0:9]:
        greet(row, c)
    for k in range(4, 8):
        greet(*neighbour(k))
    for zz in z_peers[0:3]:
        greet(index_of(mate, zz), col)

    copies = [
        pltpu.make_async_copy(tok_hbm, tok, in_sem.at[0]),
        pltpu.make_async_copy(fproj_hbm, fproj, in_sem.at[1]),
        pltpu.make_async_copy(cot_hbm, cot, in_sem.at[2]),
        pltpu.make_async_copy(fscale_hbm, fscale, in_sem.at[3]),
    ]
    for c in copies:
        c.start()
    weight_copies = [
        pltpu.make_async_copy(cproj.at[s], wxt.at[pl.ds(i * CD, CD)], w_sem.at[i])
        for i, s in enumerate((1, 2, 0))
    ]
    for c in col_peers[9:]:
        greet(row, c)
    for zz in z_peers[3:]:
        greet(index_of(mate, zz), col)
    greet((row + 2 * core - 1 + NR) % NR, col)
    for m in mates:
        greet(index_of(m, z), col)

    phase("inputs_wait")
    lane = iota((1, WIDTH), 1)
    head_mask = [jnp.where((lane >> 6) == h, 1.0, 0.0) for h in range(HEADS)]
    blocks = onehot((iota((WIDTH, WIDTH), 0) >> 6) == (iota((WIDTH, WIDTH), 1) >> 6))
    for c in copies[0:2]:
        c.wait()
    for c in weight_copies:
        c.start()
    phase("projection")
    token = tok[...]
    raw_k = mm(token, fproj[:, WIDTH : 2 * WIDTH])
    inv_k = lax.rsqrt(mm((raw_k * raw_k).astype(BF), blocks) + EPS)
    unit_k = (raw_k * inv_k).astype(BF)
    value = mm(token, fproj[:, 2 * WIDTH :]).astype(BF)
    kvx[OWN, 0:WIDTH] = unit_k
    kvx[OWN, WIDTH : 2 * WIDTH] = value
    kvx[256:288, :] = jnp.zeros((32, 2 * WIDTH), BF)
    kvx[608:640, :] = jnp.zeros((32, 2 * WIDTH), BF)

    def edge_token(slot):
        side, down, across, right, bottom, used = edge_parts(slot)
        return jnp.where(used, (down + 5 * bottom) * COLS + across + (COLS - 3) * right, -1)

    select = onehot(edge_token(iota((128, TOKENS), 0)) == iota((128, TOKENS), 1))
    staging[:, 0:WIDTH] = mm(select, unit_k).astype(BF)
    staging[:, WIDTH : 2 * WIDTH] = mm(select, value).astype(BF)
    rk_s[...] = raw_k
    ik_s[...] = inv_k

    phase("barrier_wait")
    pl.semaphore_wait(barrier, len(col_peers) + len(z_peers) + len(mates) + 5)

    phase("halo_send")
    def remote(src, dst, ss, rs, r, c):
        return pltpu.make_async_remote_copy(
            src_ref=src, dst_ref=dst, send_sem=ss, recv_sem=rs, device_id=(r, c), device_id_type=MESH
        )

    def halo_copy(k):
        o = OPPOSITE[k]
        if k == 0:
            source = kvx.at[pl.ds(OWN.start, 96)]
        elif k == 1:
            source = kvx.at[pl.ds(OWN.stop - 96, 96)]
        else:
            source = staging.at[pl.ds(START[k] - 192, LENGTH[k])]
        target = kvx.at[pl.ds(PLACE[o], LENGTH[o])]
        return remote(source, target, halo_ss.at[k], halo_rs.at[k], *neighbour(k))

    def start_all(copy):
        for k in (4, 5, 6, 7, 2, 3):
            copy(k).start()

        @pl.when(core == 0)
        def _():
            copy(0).start()
            copy(1).start()

        @pl.when(core == 1)
        def _():
            copy(1).start()
            copy(0).start()

    start_all(halo_copy)

    phase("own_attend")
    for c in copies[2:4]:
        c.wait()
    gain = sum(head_mask[h] * fscale[h] for h in range(HEADS))
    raw_q = mm(token, fproj[:, 0:WIDTH])
    inv_q = lax.rsqrt(mm((raw_q * raw_q).astype(BF), blocks) + EPS)
    unit_q = raw_q * inv_q * gain
    rq_s[...] = raw_q
    iq_s[...] = inv_q

    def head(h, size):
        return slice(h * size, (h + 1) * size)

    half_size = TOKENS // 2
    groups = [(half, pair) for half in range(2) for pair in range(2)]

    def lanes_of(half, pair):
        return head(2 * half + pair, 2 * half_size)

    for half in range(2):
        for h in range(HEADS):
            rows = unit_q[head(half, half_size), :] * head_mask[h]
            qh[head(HEADS * half + h, half_size), :] = rows.astype(BF)
    eye_s[...] = onehot(iota((WIDTH, WIDTH), 0) == iota((WIDTH, WIDTH), 1))

    def transposed(x):
        return mt(eye_s[...], x)

    def spread_heads(ref, x_t):
        for h in range(HEADS):
            rows = head(h, CD)
            for half in range(2):
                lanes = head(HEADS * half + h, half_size)
                ref[rows, lanes] = x_t[rows, head(half, half_size)].astype(BF)

    qt[...] = jnp.zeros((WIDTH, HEADS * TOKENS), BF)
    spread_heads(qt, transposed(unit_q.astype(BF)))

    def near(half, k_row, k_col):
        q = iota((1, 2 * half_size), 1)
        q_row = half * (ROWS // 2) + ((q & (half_size - 1)) >> 5)
        q_col = q & (COLS - 1)
        seen = (jnp.abs(q_row - k_row) <= 3) & (jnp.abs(q_col - k_col) <= 3)
        return jnp.where(seen, 1.0, 0.0)

    def in_image(k_row, k_col, used):
        k_row_all = k_row + row * ROWS
        k_col_all = k_col + col * COLS
        used = used & (k_row_all >= 0) & (k_row_all < ROWS * NR)
        used = used & (k_col_all >= 0) & (k_col_all < COLS * NC)
        return jnp.where(used, k_row, 1000)

    def attend(part, half, values_t, mask):
        keys = kvx[part, 0:WIDTH]
        sums, outs = [], []
        for pair in range(2):
            lanes = lanes_of(half, pair)
            e = jnp.exp(mm(keys, qt[:, lanes])) * mask
            pt[part, lanes] = e
            sums.append(jnp.sum(e, axis=0, keepdims=True))
            outs.append(mm(values_t[head(pair, 2 * CD), :], e.astype(BF)))
        return sums, outs

    values_t = transposed(value).astype(BF)
    n = iota((TOKENS, 1), 0)
    sums = []
    for half in range(2):
        new, outs = attend(OWN, half, values_t, near(half, n >> 5, n & (COLS - 1)))
        sums += new
        for pair in range(2):
            fot[head(2 * half + pair, 2 * CD), :] = outs[pair]

    phase("masks")
    def pooled(r, t):
        return (
            ((r >> 3) == (t >> 7))
            & (((r >> 2) & 1) == ((t >> 2) & 1))
            & ((r & 3) == ((t & 31) >> 3))
        )

    pool = jnp.where(pooled(iota((16, TOKENS), 0), iota((16, TOKENS), 1)), 1.0 / 16.0, 0.0).astype(BF)
    merged_tokens = mm(pool, token)
    n = iota((KEYS - TOKENS, 1), 0)
    side, down, across, right, bottom, used = edge_parts(n - 128)
    k_row = jnp.where(side, down, down - 3 + 11 * bottom)
    k_col = across - 3 + (COLS + 3) * right
    k_row = jnp.where(n < 128, ((n - 32) >> 5) - 3, jnp.where(n < 256, k_row, ((n - 256) >> 5) + ROWS))
    k_col = jnp.where((n >= 128) & (n < 256), k_col, n & (COLS - 1))
    used = (used | (n < 128) | (n >= 256)) & (n >= 32) & (n < 352)
    k_row = in_image(k_row, k_col, used)
    mask_halo = []
    for half in range(2):
        rows = slice(half * 128, half * 128 + 256)
        mask_halo.append(near(half, k_row[rows, :], k_col[rows, :]))

    phase("halo_wait")
    for k in range(8):
        halo_copy(OPPOSITE[k]).wait_recv()

    phase("halo_attend")
    halo_t = transposed(kvx[TOKENS:KEYS, WIDTH : 2 * WIDTH]).astype(BF)
    linv, outs_all = [], []
    for half in range(2):
        halo_values = halo_t[:, half * 128 : half * 128 + 256]
        more_sums, more_outs = attend(HALF_HALO[half], half, halo_values, mask_halo[half])
        for pair in range(2):
            g = 2 * half + pair
            linv.append(1.0 / (sums[g] + more_sums[pair]))
            outs_all.append((fot[head(g, 2 * CD), :] + more_outs[pair]) * linv[g])

    def join_heads(pieces):
        rows = []
        for pair in range(2):
            for h in range(2):
                blocks_of = [
                    pieces[2 * half + pair][head(h, CD), head(h, half_size)] for half in range(2)
                ]
                rows.append(jnp.concatenate(blocks_of, axis=1))
        return jnp.concatenate(rows, axis=0)

    fo_t = join_heads(outs_all).astype(BF)

    phase("merge")
    merged = merged_tokens + mt(pool, fo_t)

    def token_sum(x):
        x = x[0:8, :] + x[8:16, :]
        x = jnp.sum(x + pltpu.roll(x, 4, 0), axis=1, keepdims=True)
        return jnp.concatenate([x, x], axis=0)

    inv_m = lax.rsqrt(token_sum(merged * merged) * (1.0 / (4 * WIDTH)) + EPS)

    def part16(i):
        return pl.ds(pl.multiple_of(i * 16, 16), 16)

    cg[part16(col), :] = (merged * inv_m).astype(BF)

    phase("cn_send")
    for c in col_peers:
        remote(cg.at[part16(col)], cg.at[part16(col)], cg_ss, cg_rs, row, c).start()
    col_bytes = pl.ds(0, 16 * len(col_peers))
    cg_all = remote(cg.at[col_bytes], cg.at[col_bytes], cg_ss, cg_rs, row, col_peers[0])

    phase("cn_beside")
    mm_s[...] = merged
    inv_s[...] = inv_m
    depth = iota((CD, 4 * WIDTH), 1)
    wxt[3 * CD : 4 * CD, :] = onehot(depth == col * CD + iota((CD, 4 * WIDTH), 0))
    shift_up = onehot(iota((CD, 2 * CD), 1) == iota((CD, 2 * CD), 0) + CD)
    cot_high = mm(cot[...], shift_up)
    low_lane = iota((1, 2 * CD), 1) < CD
    for c in weight_copies:
        c.wait()
    for ab in range(4):
        wide[head(ab, WIDTH), :] = mt(eye_s[...], wxt[:, head(ab, WIDTH)]).astype(BF)
    for half, pair in groups:
        lanes = lanes_of(half, pair)
        for part in (OWN, HALF_HALO[half]):
            pt[part, lanes] = pt[part, lanes] * linv[2 * half + pair]
    for k in range(8):
        halo_copy(k).wait_send()
    phase("cn_wait")
    cg_all.wait_recv()

    phase("coarse_projection")
    part_of = (iota((16 * NC, 1), 0) >> 2) & 3
    part_mask = [jnp.where(part_of == ab, 1.0, 0.0) for ab in range(4)]
    upper_rows = iota((1, 8, 1), 1) < 4

    def by_part(x):
        return jnp.concatenate([(x * part_mask[ab]).astype(BF) for ab in range(4)], axis=1)

    made = mm(by_part(cg[...].astype(F32)), wide[...]).reshape(NC, 2, 8, 4 * CD)
    made = made[:, 0] + made[:, 1]
    made = made + pltpu.roll(made, 4, 1)
    made = made.reshape(NC // 2, 2, 8, 4 * CD)
    made = jnp.where(upper_rows, made[:, 0], made[:, 1]).reshape(CT, 4 * CD)
    made_kv = made[:, 0 : 2 * CD]
    made_qo = made[:, 2 * CD : 4 * CD]

    def low_sum(x):
        return jnp.sum(jnp.where(low_lane, x, 0.0), axis=1, keepdims=True)

    coarse_gain = cscale[0]
    inv_ck = lax.rsqrt(low_sum(made_kv * made_kv) + EPS)
    inv_cq = lax.rsqrt(low_sum(made_qo * made_qo) + EPS)
    own_kv = jnp.where(low_lane, made_kv * inv_ck, made_kv)
    own_qc = jnp.where(low_lane, made_qo * inv_cq * coarse_gain, cot_high)

    def block(i):
        return pl.ds(pl.multiple_of(i * CT, CT), CT)

    kv[block(z), :] = own_kv.astype(BF)
    qc[block(mate), :] = own_qc.astype(BF)

    phase("kv_send")
    def kv_copy(slot_of, to, d):
        return remote(
            kv.at[block(slot_of)], kv.at[block(slot_of)], kv_ss, kv_rs.at[d], index_of(mate, to), col
        )

    for d, zz in zip(z_steps, z_peers):
        kv_copy(z, zz, d).start()
    for m in mates:
        remote(qc.at[block(mate)], qc.at[block(mate)], qc_ss, qc_rs, index_of(m, z), col).start()
    z_bytes = pl.ds(0, CT * len(z_peers))
    m_bytes = pl.ds(0, CT * len(mates))
    to_z = (index_of(mate, z_peers[0]), col)
    to_mate = (index_of(mates[0], z), col)
    qc_all = remote(qc.at[m_bytes], qc.at[m_bytes], qc_ss, qc_rs, *to_mate)
    phase("kv_beside")
    cg_all.wait_send()
    for ab in range(4):
        w_kv[head(ab, 2 * CD), :] = wxt[0 : 2 * CD, head(ab, WIDTH)]
        w_qc[head(ab, 2 * CD), :] = wxt[2 * CD : 4 * CD, head(ab, WIDTH)]
    fo_s[...] = fo_t.astype(F32)
    kt[...] = transposed(kvx[:, 0:WIDTH]).astype(BF)
    for i in range(3):
        fproj_t[head(i, WIDTH), :] = transposed(fproj[:, head(i, WIDTH)]).astype(BF)
    phase("qc_wait")
    qc_all.wait_recv()
    queries = qc[...].astype(F32)
    q_low = jnp.where(low_lane, queries, 0.0).astype(BF)
    cot_only = jnp.where(low_lane, 0.0, queries).astype(BF)
    eye_small = eye_s[0 : 2 * CD, 0 : 2 * CD]
    q_low_t = mt(eye_small, q_low).astype(BF)
    cot_t = mt(eye_small, cot_only).astype(BF)

    phase("kv_scores")
    c_sum = jnp.zeros((1, NM * CT), F32)
    c_weighted = jnp.zeros((1, NM * CT), F32)
    for steps in ((0, 1, 7), (2, 6), (3, 5, 4)):
        sources = [(z + NZ - d) % NZ for d in steps]
        for d, source in zip(steps, sources):
            if d:
                kv_copy(source, source, d).wait_recv()
        some = jnp.concatenate([kv[block(source), :] for source in sources], axis=0)
        e = jnp.exp(mm(some, q_low_t))
        p = mm(some, cot_t)
        for i, source in enumerate(sources):
            ce_s[block(source), :] = e[head(i, CT), :]
            dp_s[block(source), :] = p[head(i, CT), :]
        c_sum = c_sum + jnp.sum(e, axis=0, keepdims=True)
        c_weighted = c_weighted + jnp.sum(e * p, axis=0, keepdims=True)
    phase("stats_send")
    st[mate, 0:1, :] = c_sum
    st[mate, 1:2, :] = c_weighted
    for m in mates:
        remote(st.at[mate], st.at[mate], st_ss, st_rs, index_of(m, z), col).start()
    st_bytes = pl.ds(0, len(mates))
    st_all = remote(st.at[st_bytes], st.at[st_bytes], st_ss, st_rs, *to_mate)
    phase("stats_beside")
    kv_t = mt(eye_s[0 : 2 * CD, 0 : 2 * CD], kv[...]).astype(BF)
    o_t = mm(kv_t, ce_s[...].astype(BF))
    remote(kv.at[z_bytes], kv.at[z_bytes], kv_ss, kv_rs.at[1], *to_z).wait_send()
    qc_all.wait_send()
    phase("stats_wait")
    st_all.wait_recv()
    phase("dkv_make")
    totals = (st[0] + st[1]) + (st[2] + st[3])
    c_inv = 1.0 / totals[0:1, :]
    c_delta = totals[1:2, :] * c_inv
    both = jnp.concatenate([q_low, cot_only], axis=0)
    for targets in (z_peers[0:3], z_peers[3:5], z_peers[5:7] + [z]):
        cp = jnp.concatenate([ce_s[block(zz), :] for zz in targets], axis=0) * c_inv
        cds = cp * (jnp.concatenate([dp_s[block(zz), :] for zz in targets], axis=0) - c_delta)
        cds = cds.astype(BF)
        made_here = mm(jnp.concatenate([cds, cp.astype(BF)], axis=1), both).astype(BF)
        for i, zz in enumerate(targets):
            cds_s[block(zz), :] = cds[head(i, CT), :]
            dkv[block(zz), :] = made_here[head(i, CT), :]
            if zz is not z:
                remote(
                    dkv.at[block(zz)], dkv_in.at[block(z)], dkv_ss, dkv_rs, index_of(mate, zz), col
                ).start()
    dkv_all = remote(dkv.at[z_bytes], dkv_in.at[z_bytes], dkv_ss, dkv_rs, *to_z)
    phase("dq_make")
    dq_t = mm(kv_t, cds_s[...])
    dqo_t = jnp.where(iota((2 * CD, 1), 0) < CD, dq_t, o_t * c_inv).astype(BF)
    dqo[...] = transposed(dqo_t).astype(BF)
    for m in mates:
        remote(dqo.at[block(m)], dqo_in.at[block(mate)], dqo_ss, dqo_rs, index_of(m, z), col).start()
    dqo_all = remote(dqo.at[m_bytes], dqo_in.at[m_bytes], dqo_ss, dqo_rs, *to_mate)
    dkv_in[block(z), :] = dkv[block(z), :]
    dqo_in[block(mate), :] = dqo[block(mate), :]
    st_all.wait_send()
    phase("dqo_wait")
    dqo_all.wait_recv()
    phase("dq_unit")
    d_qo = dqo_in[head(0, CT), :].astype(F32)
    for m in range(1, NM):
        d_qo = d_qo + dqo_in[head(m, CT), :].astype(F32)
    g_q = (coarse_gain * inv_cq) * (d_qo - made_qo * (inv_cq * inv_cq * low_sum(d_qo * made_qo)))

    def repeated(g):
        g = g.reshape(NC // 2, 8, 2 * CD)
        turned = pltpu.roll(g, 4, 1)
        pair = [jnp.where(upper_rows, g, turned), jnp.where(upper_rows, turned, g)]
        g = jnp.stack(pair, axis=1).reshape(NC, 1, 8, 2 * CD)
        return jnp.broadcast_to(g, (NC, 2, 8, 2 * CD)).reshape(16 * NC, 2 * CD)

    term_qc = mm(by_part(repeated(jnp.where(low_lane, g_q, cot_high))), w_qc[...])
    phase("dkv_wait")
    dkv_all.wait_recv()
    phase("term")
    d_kv = dkv_in[head(0, CT), :].astype(F32)
    for i in range(1, NZ):
        d_kv = d_kv + dkv_in[head(i, CT), :].astype(F32)
    g_k = inv_ck * (d_kv - made_kv * (inv_ck * inv_ck * low_sum(d_kv * made_kv)))
    g_kv = jnp.where(low_lane, g_k, d_kv)

    sb[...] = (term_qc + mm(by_part(repeated(g_kv)), w_kv[...])).astype(BF)
    phase("rs_send")
    for c in col_peers:
        remote(sb.at[part16(c)], rb.at[part16(col)], rs_ss, rs_rs, row, c).start()
    rs_all = remote(sb.at[col_bytes], rb.at[col_bytes], rs_ss, rs_rs, row, col_peers[0])
    phase("rs_beside")
    rb[part16(col), :] = sb[part16(col), :]
    out_c[...] = pltpu.roll(made_qo + d_qo, CD, 1)[:, 0:CD]
    dkv_all.wait_send()
    dqo_all.wait_send()
    select_s[...] = onehot(edge_token(iota((TOKENS, 128), 1)) == iota((TOKENS, 128), 0))
    spread = onehot(pooled(iota((TOKENS, 16), 1), iota((TOKENS, 16), 0)))
    dyt[...] = jnp.zeros((WIDTH, HEADS * TOKENS), BF)
    spread_t = onehot(pooled(iota((16, TOKENS), 0), iota((16, TOKENS), 1)))
    lane = iota((CD, HEADS * TOKENS), 1)
    entry = iota((CD, HEADS * TOKENS), 0)
    query = (lane >> 9) * half_size + (lane & (half_size - 1))
    collect = onehot((((lane >> 7) & 3) == (entry >> 4)) & pooled(entry & 15, query))
    sums = []
    for half in range(2):
        lanes = head(half, HEADS * half_size)
        total = [mt(pt[part, lanes].astype(BF), collect[:, lanes]) for part in (OWN, HALF_HALO[half])]
        sums.append(total)
    zeros = jnp.zeros((128, CD), F32)
    halo_sum = jnp.concatenate([sums[0][1], zeros], axis=0) + jnp.concatenate([zeros, sums[1][1]], axis=0)
    share_sum = jnp.concatenate([sums[0][0] + sums[1][0], halo_sum], axis=0)
    high = share_sum.astype(BF)
    low = (share_sum - high.astype(F32)).astype(BF)
    psum[:, 0:CD] = high
    psum[:, CD : 2 * CD] = low
    phase("rs_wait")
    rs_all.wait_recv()
    phase("norm_back")
    grad = rb[0:16, :].astype(F32)
    for c in range(1, NC):
        grad = grad + rb[head(c, 16), :].astype(F32)

    merged = mm_s[...]
    inv_m = inv_s[...]
    grad = inv_m * (grad - merged * (inv_m * inv_m * token_sum(grad * merged) * (1.0 / (4 * WIDTH))))
    dy_blocks = (grad * (1.0 / 16.0)).astype(BF)
    dy_t = mm(mt(eye_s[...], dy_blocks).astype(BF), spread_t)
    dy = mm(spread, dy_blocks)
    by_block = jnp.concatenate([dy_blocks.astype(F32) * head_mask[h] for h in range(HEADS)], axis=0).astype(BF)
    by_block = jnp.concatenate([by_block, by_block], axis=0)

    phase("halo_back")
    d_v = mm(psum[...], by_block)
    spread_heads(dyt, dy_t)
    product = dy_t * fo_s[...]
    by_head = [jnp.sum(product[head(h, CD), :], axis=0, keepdims=True) for h in range(HEADS)]
    delta = [
        jnp.concatenate([by_head[2 * pair + h][:, head(half, half_size)] for h in range(2)], axis=1)
        for half, pair in groups
    ]

    def score_side(part, half):
        values = kvx[part, WIDTH : 2 * WIDTH]
        for pair in range(2):
            lanes = lanes_of(half, pair)
            d_p = mm(values, dyt[:, lanes]) - delta[2 * half + pair]
            ds[part, lanes] = (pt[part, lanes] * d_p).astype(BF)

    def back_copy(k, source, target, i):
        o = OPPOSITE[k]
        source = source.at[pl.ds(START[k], LENGTH[k])]
        target = target.at[pl.ds(START[o], LENGTH[o])]
        return remote(source, target, back_ss.at[i], back_rs.at[i], *neighbour(k))

    def back_k(k):
        return back_copy(k, dk_halo, rh_k, k)

    def back_v(k):
        return back_copy(k, dv_halo, rh_v, 8 + k)

    dv_halo[0:96, :] = d_v[288:384, :].astype(BF)
    dv_halo[96:192, :] = d_v[512:608, :].astype(BF)
    dv_halo[192:320, :] = d_v[384:512, :].astype(BF)
    start_all(back_v)

    upper = slice(0, HEADS * half_size)
    lower = slice(HEADS * half_size, 2 * HEADS * half_size)
    score_side(HALF_HALO[0], 0)
    d_k_upper = mm(ds[HALF_HALO[0], upper], qh[upper, :])
    score_side(HALF_HALO[1], 1)
    d_k_lower = mm(ds[HALF_HALO[1], lower], qh[lower, :])
    dk_halo[192:320, :] = (d_k_upper[128:256, :] + d_k_lower[0:128, :]).astype(BF)
    dk_halo[0:96, :] = d_k_upper[32:128, :].astype(BF)
    dk_halo[96:192, :] = d_k_lower[128:224, :].astype(BF)
    start_all(back_k)

    phase("own_back")
    score_side(OWN, 0)
    score_side(OWN, 1)
    d_k = mm(ds[OWN, :], qh[...])
    d_v = d_v[OWN, :]
    phase("query_back")
    pieces = []
    for half, pair in groups:
        lanes = lanes_of(half, pair)
        from_own = mm(kt[head(pair, 2 * CD), OWN], ds[OWN, lanes])
        from_halo = mm(kt[head(pair, 2 * CD), HALF_HALO[half]], ds[HALF_HALO[half], lanes])
        pieces.append(from_own + from_halo)
    d_q = transposed(join_heads(pieces).astype(BF))
    raw_q = rq_s[...]
    inv_q = iq_s[...]
    g_q = gain * inv_q * (d_q - raw_q * (inv_q * inv_q * mm((d_q * raw_q).astype(BF), blocks)))
    result = dy + mm(g_q.astype(BF), fproj_t[0:WIDTH, :])
    rs_all.wait_send()

    phase("back_wait")
    for k in range(8):
        back_v(OPPOSITE[k]).wait_recv()

    def received(ref):
        rows = [ref[0:96, :].astype(F32), jnp.zeros((TOKENS - 192, WIDTH), F32), ref[96:192, :].astype(F32)]
        return mm(select_s[...], ref[192:320, :]) + jnp.concatenate(rows, axis=0)

    d_v = d_v + received(rh_v)
    result = result + mm(d_v.astype(BF), fproj_t[2 * WIDTH :, :])
    for k in range(8):
        back_k(OPPOSITE[k]).wait_recv()
    phase("finish")
    d_k = d_k + received(rh_k)
    raw_k = rk_s[...]
    inv_k = ik_s[...]
    g_k = inv_k * (d_k - raw_k * (inv_k * inv_k * mm((d_k * raw_k).astype(BF), blocks)))
    result = result + mm(g_k.astype(BF), fproj_t[WIDTH : 2 * WIDTH, :])
    out_f[...] = result.astype(BF)
    for k in range(8):
        back_v(k).wait_send()
        back_k(k).wait_send()
    open_scope.close()


def in_hbm(x):
    return pltpu.with_memory_space_constraint(x, pltpu.HBM)


def body(tokens, fine_proj, fine_scale, coarse_proj, coarse_scale, coarse_cot):
    vmem = pl.BlockSpec(memory_space=pltpu.VMEM)
    smem = pl.BlockSpec(memory_space=pltpu.SMEM)
    hbm = pl.BlockSpec(memory_space=pltpu.HBM)
    dma = pltpu.SemaphoreType.DMA
    out_c, out_f = pl.pallas_call(
        kernel,
        out_shape=(
            jax.ShapeDtypeStruct((CT, CD), F32),
            jax.ShapeDtypeStruct((TOKENS, WIDTH), BF),
        ),
        in_specs=[hbm, hbm, hbm, hbm, smem, hbm],
        out_specs=(vmem, vmem),
        scratch_shapes=[
            pltpu.VMEM((TOKENS, WIDTH), BF),
            pltpu.VMEM((WIDTH, 3 * WIDTH), BF),
            pltpu.SMEM((HEADS,), F32),
            pltpu.VMEM((CT, CD), BF),
            pltpu.VMEM((KEYS, 2 * WIDTH), BF),
            pltpu.VMEM((128, 2 * WIDTH), BF),
            pltpu.VMEM((TOKENS, WIDTH), F32),
            pltpu.VMEM((TOKENS, WIDTH), F32),
            pltpu.VMEM((TOKENS, WIDTH), F32),
            pltpu.VMEM((TOKENS, WIDTH), F32),
            pltpu.VMEM((HEADS * TOKENS, WIDTH), BF),
            pltpu.VMEM((WIDTH, HEADS * TOKENS), BF),
            pltpu.VMEM((KEYS, HEADS * TOKENS), F32),
            pltpu.VMEM((KEYS, 2 * CD), BF),
            pltpu.VMEM((2 * WIDTH, TOKENS), F32),
            pltpu.VMEM((TOKENS, WIDTH), F32),
            pltpu.VMEM((WIDTH, KEYS), BF),
            pltpu.VMEM((3 * WIDTH, WIDTH), BF),
            pltpu.VMEM((4 * CD, 4 * WIDTH), BF),
            pltpu.VMEM((4 * WIDTH, 4 * CD), BF),
            pltpu.VMEM((16 * NC, WIDTH), BF),
            pltpu.VMEM((16, WIDTH), F32),
            pltpu.VMEM((16, 1), F32),
            pltpu.VMEM((WIDTH, WIDTH), BF),
            pltpu.VMEM((8 * CD, WIDTH), BF),
            pltpu.VMEM((8 * CD, WIDTH), BF),
            pltpu.VMEM((TOKENS, 128), BF),
            pltpu.VMEM((NZ * CT, 2 * CD), BF),
            pltpu.VMEM((NM * CT, 2 * CD), BF),
            pltpu.VMEM((NM, 2, NM * CT), F32),
            pltpu.VMEM((NZ * CT, NM * CT), F32),
            pltpu.VMEM((NZ * CT, NM * CT), F32),
            pltpu.VMEM((NZ * CT, NM * CT), BF),
            pltpu.VMEM((NZ * CT, 2 * CD), BF),
            pltpu.VMEM((NZ * CT, 2 * CD), BF),
            pltpu.VMEM((NM * CT, 2 * CD), BF),
            pltpu.VMEM((NM * CT, 2 * CD), BF),
            pltpu.VMEM((16 * NC, WIDTH), BF),
            pltpu.VMEM((16 * NC, WIDTH), BF),
            pltpu.VMEM((WIDTH, HEADS * TOKENS), BF),
            pltpu.VMEM((KEYS, HEADS * TOKENS), BF),
            pltpu.VMEM((HALO, WIDTH), BF),
            pltpu.VMEM((HALO, WIDTH), BF),
            pltpu.VMEM((HALO, WIDTH), BF),
            pltpu.VMEM((HALO, WIDTH), BF),
            dma((4,)), dma((3,)), dma((8,)), dma((8,)),
            dma(()), dma(()), dma(()), dma((NZ,)), dma(()), dma(()), dma(()), dma(()),
            dma(()), dma(()), dma(()), dma(()), dma(()), dma(()),
            dma((16,)), dma((16,)),
        ],
        compiler_params=pltpu.CompilerParams(
            collective_id=0, has_side_effects=True, vmem_limit_bytes=40 * 1024 * 1024
        ),
        cost_estimate=pl.CostEstimate(
            flops=3_000_000_000, bytes_accessed=2_000_000, transcendentals=1_000_000
        ),
        name="hourglass",
    )(
        in_hbm(tokens.reshape(TOKENS, WIDTH)),
        in_hbm(fine_proj),
        in_hbm(fine_scale),
        in_hbm(jnp.swapaxes(coarse_proj, 1, 2)),
        coarse_scale,
        in_hbm(coarse_cot.reshape(CT, CD)),
    )
    return out_c.reshape(1, CT, CD), out_f.reshape(ROWS, COLS, WIDTH)


def solution(mesh):
    return jax.shard_map(
        body,
        mesh=mesh,
        in_specs=(
            P("row", "col", None),
            P(),
            P(),
            P(None, None, "col"),
            P("col"),
            P("row", None, "col"),
        ),
        out_specs=(P("row", None, "col"), P("row", "col", None)),
        check_vma=False,
    )
```

```python
import contextlib

import jax
import jax.numpy as jnp
from jax import lax
from jax.experimental import pallas as pl
from jax.experimental.pallas import tpu as pltpu
from jax.sharding import PartitionSpec as P

F32 = jnp.float32
BF = jnp.bfloat16
I32 = jnp.int32
EPS = 1e-06
MESH = pl.DeviceIdType.MESH

NY, NZ, NCORE = 2, 8, 2
NR, NC = NY * NZ * NCORE, 16
ROWS, COLS, WIDTH, HEADS = 8, 32, 256, 4
TOKENS = ROWS * COLS
HALO = 320
KEYS = 640
OWN = slice(0, 256)
HALF_HALO = (slice(256, 512), slice(384, 640))
CT = 4 * NC
CD = 64
NM = NY * NCORE

DIRS = ((-1, 0), (1, 0), (0, -1), (0, 1), (-1, -1), (-1, 1), (1, -1), (1, 1))
OPPOSITE = (1, 0, 3, 2, 7, 6, 5, 4)
START = (0, 96, 192, 224, 256, 272, 288, 304)
PLACE = (288, 512, 384, 416, 448, 464, 480, 496)
LENGTH = (96, 96, 32, 32, 16, 16, 16, 16)


def mm(a, b):
    return jnp.dot(a, b, preferred_element_type=F32)


def mt(a, b):
    return lax.dot_general(a, b, (((1,), (1,)), ((), ())), preferred_element_type=F32)


def iota(shape, dim):
    return lax.broadcasted_iota(I32, shape, dim)


def onehot(condition):
    return jnp.where(condition, 1.0, 0.0).astype(BF)


def third(m):
    return (m * 11) >> 5


def edge_parts(p):
    side = p < 64
    m = jnp.where(side, p & 31, p & 15)
    down = third(m)
    across = m - 3 * down
    right = jnp.where(side, (p >> 5) & 1, (p >> 4) & 1)
    bottom = jnp.where(side, 0, ((p - 64) >> 5) & 1)
    used = m < jnp.where(side, 24, 9)
    return side, down, across, right, bottom, used


def kernel(
    tok_hbm, fproj_hbm, fscale_hbm, cproj, cscale, cot_hbm,
    out_c, out_f,
    tok, fproj, fscale, cot, kvx, halo_tok, staging, rq_s, rk_s, iq_s, ik_s, qh, qt, pt, psum, fot, fo_s, kt, fproj_t, wxt, wide, cg, mm_s, inv_s,
    eye_s, w_kv, w_qc, select_s,
    kv, qc, st, ce_s, dp_s, cds_s, dkv, dkv_in, dqo, dqo_in, sb, rb, dyt, ds, dg_halo, rh,
    in_sem, w_sem, halo_ss, halo_rs, cg_ss, cg_rs, kv_ss, kv_rs, qc_ss, qc_rs, st_ss, st_rs,
    dkv_ss, dkv_rs, dqo_ss, dqo_rs, rs_ss, rs_rs, back_ss, back_rs,
):
    row = lax.axis_index("row")
    col = lax.axis_index("col")
    core = row % NCORE
    z = (row // NCORE) % NZ
    y = row // (NCORE * NZ)
    mate = y * NCORE + core
    col_hi = col // 4
    col_lo = col % 4

    def index_of(m, zz):
        return ((m // NCORE) * NZ + zz) * NCORE + m % NCORE

    def neighbour(k):
        return (row + DIRS[k][0] + NR) % NR, (col + DIRS[k][1] + NC) % NC

    z_steps = (4, 3, 5, 2, 6, 1, 7)
    col_steps = sorted(
        ((hi, lo) for hi in range(4) for lo in range(4) if (hi, lo) != (0, 0)),
        key=lambda s: -(2 * min(s[0], 4 - s[0]) + min(s[1], 4 - s[1])),
    )
    z_peers = [(z + d) % NZ for d in z_steps]
    mates = [(mate + d) % NM for d in range(1, NM)]
    col_peers = [((col_hi + hi) % 4) * 4 + (col_lo + lo) % 4 for hi, lo in col_steps]

    open_scope = contextlib.ExitStack()

    def phase(name):
        open_scope.close()
        open_scope.enter_context(jax.named_scope(name))

    barrier = pltpu.get_barrier_semaphore()

    def greet(r, c):
        pl.semaphore_signal(barrier, inc=1, device_id=(r, c), device_id_type=MESH)

    phase("greet")
    for c in col_peers[0:9]:
        greet(row, c)
    for k in range(4, 8):
        greet(*neighbour(k))
    for zz in z_peers[0:3]:
        greet(index_of(mate, zz), col)

    copies = [
        pltpu.make_async_copy(tok_hbm, tok, in_sem.at[0]),
        pltpu.make_async_copy(fproj_hbm, fproj, in_sem.at[1]),
        pltpu.make_async_copy(cot_hbm, cot, in_sem.at[2]),
        pltpu.make_async_copy(fscale_hbm, fscale, in_sem.at[3]),
    ]
    for c in copies:
        c.start()
    weight_copies = [
        pltpu.make_async_copy(cproj.at[s], wxt.at[pl.ds(i * CD, CD)], w_sem.at[i])
        for i, s in enumerate((1, 2, 0))
    ]
    for c in col_peers[9:]:
        greet(row, c)
    for zz in z_peers[3:]:
        greet(index_of(mate, zz), col)
    greet((row + 2 * core - 1 + NR) % NR, col)
    for m in mates:
        greet(index_of(m, z), col)

    phase("inputs_wait")
    def edge_token(slot):
        side, down, across, right, bottom, used = edge_parts(slot)
        return jnp.where(used, (down + 5 * bottom) * COLS + across + (COLS - 3) * right, -1)

    select = onehot(edge_token(iota((128, TOKENS), 0)) == iota((128, TOKENS), 1))
    copies[0].wait()
    token = tok[...]
    staging[...] = mm(select, token).astype(BF)
    nothing = jnp.zeros((32, WIDTH), BF)
    halo_tok[0:32, :] = nothing
    halo_tok[KEYS - TOKENS - 32 :, :] = nothing
    phase("barrier_wait")
    pl.semaphore_wait(barrier, len(col_peers) + len(z_peers) + len(mates) + 5)

    def remote(src, dst, ss, rs, r, c):
        return pltpu.make_async_remote_copy(
            src_ref=src, dst_ref=dst, send_sem=ss, recv_sem=rs, device_id=(r, c), device_id_type=MESH
        )

    def halo_copy(k):
        o = OPPOSITE[k]
        if k == 0:
            source = tok.at[pl.ds(0, 96)]
        elif k == 1:
            source = tok.at[pl.ds(TOKENS - 96, 96)]
        else:
            source = staging.at[pl.ds(START[k] - 192, LENGTH[k])]
        target = halo_tok.at[pl.ds(PLACE[o] - TOKENS, LENGTH[o])]
        return remote(source, target, halo_ss.at[k], halo_rs.at[k], *neighbour(k))

    for k in (4, 5, 6, 7, 2, 3, 0, 1):
        halo_copy(k).start()

    phase("own_attend")
    for c in copies[1:4]:
        c.wait()
    for c in weight_copies:
        c.start()
    lane = iota((1, WIDTH), 1)
    head_mask = [jnp.where((lane >> 6) == h, 1.0, 0.0) for h in range(HEADS)]
    blocks = onehot((iota((WIDTH, WIDTH), 0) >> 6) == (iota((WIDTH, WIDTH), 1) >> 6))

    def project(x):
        raw = mm(x, fproj[:, WIDTH : 2 * WIDTH])
        inv = lax.rsqrt(mm((raw * raw).astype(BF), blocks) + EPS)
        return raw, inv, mm(x, fproj[:, 2 * WIDTH :]).astype(BF)

    raw_k, inv_k, value = project(token)
    kvx[OWN, 0:WIDTH] = (raw_k * inv_k).astype(BF)
    kvx[OWN, WIDTH : 2 * WIDTH] = value
    rk_s[...] = raw_k
    ik_s[...] = inv_k
    gain = sum(head_mask[h] * fscale[h] for h in range(HEADS))
    raw_q = mm(token, fproj[:, 0:WIDTH])
    inv_q = lax.rsqrt(mm((raw_q * raw_q).astype(BF), blocks) + EPS)
    unit_q = raw_q * inv_q * gain
    rq_s[...] = raw_q
    iq_s[...] = inv_q

    def head(h, size):
        return slice(h * size, (h + 1) * size)

    half_size = TOKENS // 2
    groups = [(half, pair) for half in range(2) for pair in range(2)]

    def lanes_of(half, pair):
        return head(2 * half + pair, 2 * half_size)

    for half in range(2):
        for h in range(HEADS):
            rows = unit_q[head(half, half_size), :] * head_mask[h]
            qh[head(HEADS * half + h, half_size), :] = rows.astype(BF)
    eye_s[...] = onehot(iota((WIDTH, WIDTH), 0) == iota((WIDTH, WIDTH), 1))

    def transposed(x):
        return mt(eye_s[...], x)

    def spread_heads(ref, x_t):
        for h in range(HEADS):
            rows = head(h, CD)
            for half in range(2):
                lanes = head(HEADS * half + h, half_size)
                ref[rows, lanes] = x_t[rows, head(half, half_size)].astype(BF)

    qt[...] = jnp.zeros((WIDTH, HEADS * TOKENS), BF)
    spread_heads(qt, transposed(unit_q.astype(BF)))

    def near(half, k_row, k_col):
        q = iota((1, 2 * half_size), 1)
        q_row = half * (ROWS // 2) + ((q & (half_size - 1)) >> 5)
        q_col = q & (COLS - 1)
        seen = (jnp.abs(q_row - k_row) <= 3) & (jnp.abs(q_col - k_col) <= 3)
        return jnp.where(seen, 1.0, 0.0)

    def in_image(k_row, k_col, used):
        k_row_all = k_row + row * ROWS
        k_col_all = k_col + col * COLS
        used = used & (k_row_all >= 0) & (k_row_all < ROWS * NR)
        used = used & (k_col_all >= 0) & (k_col_all < COLS * NC)
        return jnp.where(used, k_row, 1000)

    def attend(part, half, values_t, mask):
        keys = kvx[part, 0:WIDTH]
        sums, outs = [], []
        for pair in range(2):
            lanes = lanes_of(half, pair)
            e = jnp.exp(mm(keys, qt[:, lanes])) * mask
            pt[part, lanes] = e
            sums.append(jnp.sum(e, axis=0, keepdims=True))
            outs.append(mm(values_t[head(pair, 2 * CD), :], e.astype(BF)))
        return sums, outs

    values_t = transposed(value).astype(BF)
    n = iota((TOKENS, 1), 0)
    sums = []
    for half in range(2):
        new, outs = attend(OWN, half, values_t, near(half, n >> 5, n & (COLS - 1)))
        sums += new
        for pair in range(2):
            fot[head(2 * half + pair, 2 * CD), :] = outs[pair]

    phase("masks")
    def pooled(r, t):
        return (
            ((r >> 3) == (t >> 7))
            & (((r >> 2) & 1) == ((t >> 2) & 1))
            & ((r & 3) == ((t & 31) >> 3))
        )

    pool = jnp.where(pooled(iota((16, TOKENS), 0), iota((16, TOKENS), 1)), 1.0 / 16.0, 0.0).astype(BF)
    merged_tokens = mm(pool, token)
    n = iota((KEYS - TOKENS, 1), 0)
    side, down, across, right, bottom, used = edge_parts(n - 128)
    k_row = jnp.where(side, down, down - 3 + 11 * bottom)
    k_col = across - 3 + (COLS + 3) * right
    k_row = jnp.where(n < 128, ((n - 32) >> 5) - 3, jnp.where(n < 256, k_row, ((n - 256) >> 5) + ROWS))
    k_col = jnp.where((n >= 128) & (n < 256), k_col, n & (COLS - 1))
    used = (used | (n < 128) | (n >= 256)) & (n >= 32) & (n < 352)
    k_row = in_image(k_row, k_col, used)
    mask_halo = []
    for half in range(2):
        rows = slice(half * 128, half * 128 + 256)
        mask_halo.append(near(half, k_row[rows, :], k_col[rows, :]))

    phase("halo_wait")
    for k in range(8):
        halo_copy(OPPOSITE[k]).wait_recv()

    phase("halo_attend")
    raw_halo, inv_halo, halo_value = project(halo_tok[...])
    kvx[TOKENS:KEYS, 0:WIDTH] = (raw_halo * inv_halo).astype(BF)
    kvx[TOKENS:KEYS, WIDTH : 2 * WIDTH] = halo_value
    halo_t = transposed(halo_value).astype(BF)
    linv, outs_all = [], []
    for half in range(2):
        halo_values = halo_t[:, half * 128 : half * 128 + 256]
        more_sums, more_outs = attend(HALF_HALO[half], half, halo_values, mask_halo[half])
        for pair in range(2):
            g = 2 * half + pair
            linv.append(1.0 / (sums[g] + more_sums[pair]))
            outs_all.append((fot[head(g, 2 * CD), :] + more_outs[pair]) * linv[g])

    def join_heads(pieces):
        rows = []
        for pair in range(2):
            for h in range(2):
                blocks_of = [
                    pieces[2 * half + pair][head(h, CD), head(h, half_size)] for half in range(2)
                ]
                rows.append(jnp.concatenate(blocks_of, axis=1))
        return jnp.concatenate(rows, axis=0)

    fo_t = join_heads(outs_all).astype(BF)

    phase("merge")
    merged = merged_tokens + mt(pool, fo_t)

    def token_sum(x):
        x = x[0:8, :] + x[8:16, :]
        x = jnp.sum(x + pltpu.roll(x, 4, 0), axis=1, keepdims=True)
        return jnp.concatenate([x, x], axis=0)

    inv_m = lax.rsqrt(token_sum(merged * merged) * (1.0 / (4 * WIDTH)) + EPS)

    def part16(i):
        return pl.ds(pl.multiple_of(i * 16, 16), 16)

    cg[part16(col), :] = (merged * inv_m).astype(BF)

    phase("cn_send")
    for c in col_peers:
        remote(cg.at[part16(col)], cg.at[part16(col)], cg_ss, cg_rs, row, c).start()
    col_bytes = pl.ds(0, 16 * len(col_peers))
    cg_all = remote(cg.at[col_bytes], cg.at[col_bytes], cg_ss, cg_rs, row, col_peers[0])

    phase("cn_beside")
    mm_s[...] = merged
    inv_s[...] = inv_m
    depth = iota((CD, 4 * WIDTH), 1)
    wxt[3 * CD : 4 * CD, :] = onehot(depth == col * CD + iota((CD, 4 * WIDTH), 0))
    shift_up = onehot(iota((CD, 2 * CD), 1) == iota((CD, 2 * CD), 0) + CD)
    cot_high = mm(cot[...], shift_up)
    low_lane = iota((1, 2 * CD), 1) < CD
    for c in weight_copies:
        c.wait()
    for ab in range(4):
        wide[head(ab, WIDTH), :] = mt(eye_s[...], wxt[:, head(ab, WIDTH)]).astype(BF)
    for half, pair in groups:
        lanes = lanes_of(half, pair)
        for part in (OWN, HALF_HALO[half]):
            pt[part, lanes] = pt[part, lanes] * linv[2 * half + pair]
    for k in range(8):
        halo_copy(k).wait_send()
    phase("cn_wait")
    cg_all.wait_recv()

    phase("coarse_projection")
    part_of = (iota((16 * NC, 1), 0) >> 2) & 3
    part_mask = [jnp.where(part_of == ab, 1.0, 0.0) for ab in range(4)]
    upper_rows = iota((1, 8, 1), 1) < 4

    def by_part(x):
        return jnp.concatenate([(x * part_mask[ab]).astype(BF) for ab in range(4)], axis=1)

    made = mm(by_part(cg[...].astype(F32)), wide[...]).reshape(NC, 2, 8, 4 * CD)
    made = made[:, 0] + made[:, 1]
    made = made + pltpu.roll(made, 4, 1)
    made = made.reshape(NC // 2, 2, 8, 4 * CD)
    made = jnp.where(upper_rows, made[:, 0], made[:, 1]).reshape(CT, 4 * CD)
    made_kv = made[:, 0 : 2 * CD]
    made_qo = made[:, 2 * CD : 4 * CD]

    def low_sum(x):
        return jnp.sum(jnp.where(low_lane, x, 0.0), axis=1, keepdims=True)

    coarse_gain = cscale[0]
    inv_ck = lax.rsqrt(low_sum(made_kv * made_kv) + EPS)
    inv_cq = lax.rsqrt(low_sum(made_qo * made_qo) + EPS)
    own_kv = jnp.where(low_lane, made_kv * inv_ck, made_kv)
    own_qc = jnp.where(low_lane, made_qo * inv_cq * coarse_gain, cot_high)

    def block(i):
        return pl.ds(pl.multiple_of(i * CT, CT), CT)

    kv[block(z), :] = own_kv.astype(BF)
    qc[block(mate), :] = own_qc.astype(BF)

    phase("kv_send")
    def kv_copy(slot_of, to, d):
        return remote(
            kv.at[block(slot_of)], kv.at[block(slot_of)], kv_ss, kv_rs.at[d], index_of(mate, to), col
        )

    for d, zz in zip(z_steps, z_peers):
        kv_copy(z, zz, d).start()
    for m in mates:
        remote(qc.at[block(mate)], qc.at[block(mate)], qc_ss, qc_rs, index_of(m, z), col).start()
    z_bytes = pl.ds(0, CT * len(z_peers))
    m_bytes = pl.ds(0, CT * len(mates))
    to_z = (index_of(mate, z_peers[0]), col)
    to_mate = (index_of(mates[0], z), col)
    qc_all = remote(qc.at[m_bytes], qc.at[m_bytes], qc_ss, qc_rs, *to_mate)
    phase("kv_beside")
    cg_all.wait_send()
    for ab in range(4):
        w_kv[head(ab, 2 * CD), :] = wxt[0 : 2 * CD, head(ab, WIDTH)]
        w_qc[head(ab, 2 * CD), :] = wxt[2 * CD : 4 * CD, head(ab, WIDTH)]
    fo_s[...] = fo_t.astype(F32)
    kt[...] = transposed(kvx[:, 0:WIDTH]).astype(BF)
    for i in range(3):
        fproj_t[head(i, WIDTH), :] = transposed(fproj[:, head(i, WIDTH)]).astype(BF)
    phase("qc_wait")
    qc_all.wait_recv()
    queries = qc[...].astype(F32)
    q_low = jnp.where(low_lane, queries, 0.0).astype(BF)
    cot_only = jnp.where(low_lane, 0.0, queries).astype(BF)
    eye_small = eye_s[0 : 2 * CD, 0 : 2 * CD]
    q_low_t = mt(eye_small, q_low).astype(BF)
    cot_t = mt(eye_small, cot_only).astype(BF)

    phase("kv_scores")
    c_sum = jnp.zeros((1, NM * CT), F32)
    c_weighted = jnp.zeros((1, NM * CT), F32)
    for steps in ((0, 1, 7), (2, 6), (3, 5, 4)):
        sources = [(z + NZ - d) % NZ for d in steps]
        for d, source in zip(steps, sources):
            if d:
                kv_copy(source, source, d).wait_recv()
        some = jnp.concatenate([kv[block(source), :] for source in sources], axis=0)
        e = jnp.exp(mm(some, q_low_t))
        p = mm(some, cot_t)
        for i, source in enumerate(sources):
            ce_s[block(source), :] = e[head(i, CT), :]
            dp_s[block(source), :] = p[head(i, CT), :]
        c_sum = c_sum + jnp.sum(e, axis=0, keepdims=True)
        c_weighted = c_weighted + jnp.sum(e * p, axis=0, keepdims=True)
    phase("stats_send")
    st[mate, 0:1, :] = c_sum
    st[mate, 1:2, :] = c_weighted
    for m in mates:
        remote(st.at[mate], st.at[mate], st_ss, st_rs, index_of(m, z), col).start()
    st_bytes = pl.ds(0, len(mates))
    st_all = remote(st.at[st_bytes], st.at[st_bytes], st_ss, st_rs, *to_mate)
    phase("stats_beside")
    kv_t = mt(eye_s[0 : 2 * CD, 0 : 2 * CD], kv[...]).astype(BF)
    o_t = mm(kv_t, ce_s[...].astype(BF))
    remote(kv.at[z_bytes], kv.at[z_bytes], kv_ss, kv_rs.at[1], *to_z).wait_send()
    qc_all.wait_send()
    phase("stats_wait")
    st_all.wait_recv()
    phase("dkv_make")
    totals = (st[0] + st[1]) + (st[2] + st[3])
    c_inv = 1.0 / totals[0:1, :]
    c_delta = totals[1:2, :] * c_inv
    both = jnp.concatenate([q_low, cot_only], axis=0)
    for targets in (z_peers[0:3], z_peers[3:5], z_peers[5:7] + [z]):
        cp = jnp.concatenate([ce_s[block(zz), :] for zz in targets], axis=0) * c_inv
        cds = cp * (jnp.concatenate([dp_s[block(zz), :] for zz in targets], axis=0) - c_delta)
        cds = cds.astype(BF)
        made_here = mm(jnp.concatenate([cds, cp.astype(BF)], axis=1), both).astype(BF)
        for i, zz in enumerate(targets):
            cds_s[block(zz), :] = cds[head(i, CT), :]
            dkv[block(zz), :] = made_here[head(i, CT), :]
            if zz is not z:
                remote(
                    dkv.at[block(zz)], dkv_in.at[block(z)], dkv_ss, dkv_rs, index_of(mate, zz), col
                ).start()
    dkv_all = remote(dkv.at[z_bytes], dkv_in.at[z_bytes], dkv_ss, dkv_rs, *to_z)
    phase("dq_make")
    dq_t = mm(kv_t, cds_s[...])
    dqo_t = jnp.where(iota((2 * CD, 1), 0) < CD, dq_t, o_t * c_inv).astype(BF)
    dqo[...] = transposed(dqo_t).astype(BF)
    for m in mates:
        remote(dqo.at[block(m)], dqo_in.at[block(mate)], dqo_ss, dqo_rs, index_of(m, z), col).start()
    dqo_all = remote(dqo.at[m_bytes], dqo_in.at[m_bytes], dqo_ss, dqo_rs, *to_mate)
    dkv_in[block(z), :] = dkv[block(z), :]
    dqo_in[block(mate), :] = dqo[block(mate), :]
    st_all.wait_send()
    phase("dqo_wait")
    dqo_all.wait_recv()
    phase("dq_unit")
    d_qo = dqo_in[head(0, CT), :].astype(F32)
    for m in range(1, NM):
        d_qo = d_qo + dqo_in[head(m, CT), :].astype(F32)
    g_q = (coarse_gain * inv_cq) * (d_qo - made_qo * (inv_cq * inv_cq * low_sum(d_qo * made_qo)))

    def repeated(g):
        g = g.reshape(NC // 2, 8, 2 * CD)
        turned = pltpu.roll(g, 4, 1)
        pair = [jnp.where(upper_rows, g, turned), jnp.where(upper_rows, turned, g)]
        g = jnp.stack(pair, axis=1).reshape(NC, 1, 8, 2 * CD)
        return jnp.broadcast_to(g, (NC, 2, 8, 2 * CD)).reshape(16 * NC, 2 * CD)

    term_qc = mm(by_part(repeated(jnp.where(low_lane, g_q, cot_high))), w_qc[...])
    phase("dkv_wait")
    dkv_all.wait_recv()
    phase("term")
    d_kv = dkv_in[head(0, CT), :].astype(F32)
    for i in range(1, NZ):
        d_kv = d_kv + dkv_in[head(i, CT), :].astype(F32)
    g_k = inv_ck * (d_kv - made_kv * (inv_ck * inv_ck * low_sum(d_kv * made_kv)))
    g_kv = jnp.where(low_lane, g_k, d_kv)

    sb[...] = (term_qc + mm(by_part(repeated(g_kv)), w_kv[...])).astype(BF)
    phase("rs_send")
    for c in col_peers:
        remote(sb.at[part16(c)], rb.at[part16(col)], rs_ss, rs_rs, row, c).start()
    rs_all = remote(sb.at[col_bytes], rb.at[col_bytes], rs_ss, rs_rs, row, col_peers[0])
    phase("rs_beside")
    rb[part16(col), :] = sb[part16(col), :]
    out_c[...] = pltpu.roll(made_qo + d_qo, CD, 1)[:, 0:CD]
    dkv_all.wait_send()
    dqo_all.wait_send()
    select_s[...] = onehot(edge_token(iota((TOKENS, 128), 1)) == iota((TOKENS, 128), 0))
    spread = onehot(pooled(iota((TOKENS, 16), 1), iota((TOKENS, 16), 0)))
    dyt[...] = jnp.zeros((WIDTH, HEADS * TOKENS), BF)
    spread_t = onehot(pooled(iota((16, TOKENS), 0), iota((16, TOKENS), 1)))
    lane = iota((CD, HEADS * TOKENS), 1)
    entry = iota((CD, HEADS * TOKENS), 0)
    query = (lane >> 9) * half_size + (lane & (half_size - 1))
    collect = onehot((((lane >> 7) & 3) == (entry >> 4)) & pooled(entry & 15, query))
    sums = []
    for half in range(2):
        lanes = head(half, HEADS * half_size)
        total = [mt(pt[part, lanes].astype(BF), collect[:, lanes]) for part in (OWN, HALF_HALO[half])]
        sums.append(total)
    zeros = jnp.zeros((128, CD), F32)
    halo_sum = jnp.concatenate([sums[0][1], zeros], axis=0) + jnp.concatenate([zeros, sums[1][1]], axis=0)
    share_sum = jnp.concatenate([sums[0][0] + sums[1][0], halo_sum], axis=0)
    high = share_sum.astype(BF)
    low = (share_sum - high.astype(F32)).astype(BF)
    psum[:, 0:CD] = high
    psum[:, CD : 2 * CD] = low
    phase("rs_wait")
    rs_all.wait_recv()
    phase("norm_back")
    grad = rb[0:16, :].astype(F32)
    for c in range(1, NC):
        grad = grad + rb[head(c, 16), :].astype(F32)

    merged = mm_s[...]
    inv_m = inv_s[...]
    grad = inv_m * (grad - merged * (inv_m * inv_m * token_sum(grad * merged) * (1.0 / (4 * WIDTH))))
    dy_blocks = (grad * (1.0 / 16.0)).astype(BF)
    dy_t = mm(mt(eye_s[...], dy_blocks).astype(BF), spread_t)
    dy = mm(spread, dy_blocks)
    by_block = jnp.concatenate([dy_blocks.astype(F32) * head_mask[h] for h in range(HEADS)], axis=0).astype(BF)
    by_block = jnp.concatenate([by_block, by_block], axis=0)

    phase("halo_back")
    spread_heads(dyt, dy_t)
    product = dy_t * fo_s[...]
    by_head = [jnp.sum(product[head(h, CD), :], axis=0, keepdims=True) for h in range(HEADS)]
    delta = [
        jnp.concatenate([by_head[2 * pair + h][:, head(half, half_size)] for h in range(2)], axis=1)
        for half, pair in groups
    ]

    def score_side(part, half):
        values = kvx[part, WIDTH : 2 * WIDTH]
        for pair in range(2):
            lanes = lanes_of(half, pair)
            d_p = mm(values, dyt[:, lanes]) - delta[2 * half + pair]
            ds[part, lanes] = (pt[part, lanes] * d_p).astype(BF)

    d_v = mm(psum[...], by_block)
    dg_halo[0:96, WIDTH : 2 * WIDTH] = d_v[288:384, :].astype(BF)
    dg_halo[96:192, WIDTH : 2 * WIDTH] = d_v[512:608, :].astype(BF)
    dg_halo[192:320, WIDTH : 2 * WIDTH] = d_v[384:512, :].astype(BF)

    def back_copy(k):
        o = OPPOSITE[k]
        source = dg_halo.at[pl.ds(START[k], LENGTH[k])]
        target = rh.at[pl.ds(START[o], LENGTH[o])]
        return remote(source, target, back_ss.at[k], back_rs.at[k], *neighbour(k))

    upper = slice(0, HEADS * half_size)
    lower = slice(HEADS * half_size, 2 * HEADS * half_size)
    score_side(HALF_HALO[0], 0)
    d_k_upper = mm(ds[HALF_HALO[0], upper], qh[upper, :])
    score_side(HALF_HALO[1], 1)
    d_k_lower = mm(ds[HALF_HALO[1], lower], qh[lower, :])
    dg_halo[192:320, 0:WIDTH] = (d_k_upper[128:256, :] + d_k_lower[0:128, :]).astype(BF)
    for k in (4, 5, 6, 7, 2, 3):
        back_copy(k).start()
    dg_halo[0:96, 0:WIDTH] = d_k_upper[32:128, :].astype(BF)
    back_copy(0).start()
    dg_halo[96:192, 0:WIDTH] = d_k_lower[128:224, :].astype(BF)
    back_copy(1).start()

    phase("own_back")
    score_side(OWN, 0)
    score_side(OWN, 1)
    d_k = mm(ds[OWN, :], qh[...])
    d_v = d_v[OWN, :]
    phase("query_back")
    pieces = []
    for half, pair in groups:
        lanes = lanes_of(half, pair)
        from_own = mm(kt[head(pair, 2 * CD), OWN], ds[OWN, lanes])
        from_halo = mm(kt[head(pair, 2 * CD), HALF_HALO[half]], ds[HALF_HALO[half], lanes])
        pieces.append(from_own + from_halo)
    d_q = transposed(join_heads(pieces).astype(BF))
    raw_q = rq_s[...]
    inv_q = iq_s[...]
    g_q = gain * inv_q * (d_q - raw_q * (inv_q * inv_q * mm((d_q * raw_q).astype(BF), blocks)))
    result = dy + mm(g_q.astype(BF), fproj_t[0:WIDTH, :])
    rs_all.wait_send()

    phase("back_wait")
    for k in range(8):
        back_copy(OPPOSITE[k]).wait_recv()
    phase("finish")
    received = mm(select_s[...], rh[192:320, :]) + jnp.concatenate(
        [
            rh[0:96, :].astype(F32),
            jnp.zeros((TOKENS - 192, 2 * WIDTH), F32),
            rh[96:192, :].astype(F32),
        ],
        axis=0,
    )
    d_k = d_k + received[:, 0:WIDTH]
    d_v = d_v + received[:, WIDTH : 2 * WIDTH]
    raw_k = rk_s[...]
    inv_k = ik_s[...]
    g_k = inv_k * (d_k - raw_k * (inv_k * inv_k * mm((d_k * raw_k).astype(BF), blocks)))
    g_kv = jnp.concatenate([g_k.astype(BF), d_v.astype(BF)], axis=1)
    result = result + mm(g_kv, fproj_t[WIDTH:, :])
    out_f[...] = result.astype(BF)
    for k in range(8):
        back_copy(k).wait_send()
    open_scope.close()


def in_hbm(x):
    return pltpu.with_memory_space_constraint(x, pltpu.HBM)


def body(tokens, fine_proj, fine_scale, coarse_proj, coarse_scale, coarse_cot):
    vmem = pl.BlockSpec(memory_space=pltpu.VMEM)
    smem = pl.BlockSpec(memory_space=pltpu.SMEM)
    hbm = pl.BlockSpec(memory_space=pltpu.HBM)
    dma = pltpu.SemaphoreType.DMA
    out_c, out_f = pl.pallas_call(
        kernel,
        out_shape=(
            jax.ShapeDtypeStruct((CT, CD), F32),
            jax.ShapeDtypeStruct((TOKENS, WIDTH), BF),
        ),
        in_specs=[hbm, hbm, hbm, hbm, smem, hbm],
        out_specs=(vmem, vmem),
        scratch_shapes=[
            pltpu.VMEM((TOKENS, WIDTH), BF),
            pltpu.VMEM((WIDTH, 3 * WIDTH), BF),
            pltpu.SMEM((HEADS,), F32),
            pltpu.VMEM((CT, CD), BF),
            pltpu.VMEM((KEYS, 2 * WIDTH), BF),
            pltpu.VMEM((KEYS - TOKENS, WIDTH), BF),
            pltpu.VMEM((128, WIDTH), BF),
            pltpu.VMEM((TOKENS, WIDTH), F32),
            pltpu.VMEM((TOKENS, WIDTH), F32),
            pltpu.VMEM((TOKENS, WIDTH), F32),
            pltpu.VMEM((TOKENS, WIDTH), F32),
            pltpu.VMEM((HEADS * TOKENS, WIDTH), BF),
            pltpu.VMEM((WIDTH, HEADS * TOKENS), BF),
            pltpu.VMEM((KEYS, HEADS * TOKENS), F32),
            pltpu.VMEM((KEYS, 2 * CD), BF),
            pltpu.VMEM((2 * WIDTH, TOKENS), F32),
            pltpu.VMEM((TOKENS, WIDTH), F32),
            pltpu.VMEM((WIDTH, KEYS), BF),
            pltpu.VMEM((3 * WIDTH, WIDTH), BF),
            pltpu.VMEM((4 * CD, 4 * WIDTH), BF),
            pltpu.VMEM((4 * WIDTH, 4 * CD), BF),
            pltpu.VMEM((16 * NC, WIDTH), BF),
            pltpu.VMEM((16, WIDTH), F32),
            pltpu.VMEM((16, 1), F32),
            pltpu.VMEM((WIDTH, WIDTH), BF),
            pltpu.VMEM((8 * CD, WIDTH), BF),
            pltpu.VMEM((8 * CD, WIDTH), BF),
            pltpu.VMEM((TOKENS, 128), BF),
            pltpu.VMEM((NZ * CT, 2 * CD), BF),
            pltpu.VMEM((NM * CT, 2 * CD), BF),
            pltpu.VMEM((NM, 2, NM * CT), F32),
            pltpu.VMEM((NZ * CT, NM * CT), F32),
            pltpu.VMEM((NZ * CT, NM * CT), F32),
            pltpu.VMEM((NZ * CT, NM * CT), BF),
            pltpu.VMEM((NZ * CT, 2 * CD), BF),
            pltpu.VMEM((NZ * CT, 2 * CD), BF),
            pltpu.VMEM((NM * CT, 2 * CD), BF),
            pltpu.VMEM((NM * CT, 2 * CD), BF),
            pltpu.VMEM((16 * NC, WIDTH), BF),
            pltpu.VMEM((16 * NC, WIDTH), BF),
            pltpu.VMEM((WIDTH, HEADS * TOKENS), BF),
            pltpu.VMEM((KEYS, HEADS * TOKENS), BF),
            pltpu.VMEM((HALO, 2 * WIDTH), BF),
            pltpu.VMEM((HALO, 2 * WIDTH), BF),
            dma((4,)), dma((3,)), dma((8,)), dma((8,)),
            dma(()), dma(()), dma(()), dma((NZ,)), dma(()), dma(()), dma(()), dma(()),
            dma(()), dma(()), dma(()), dma(()), dma(()), dma(()),
            dma((8,)), dma((8,)),
        ],
        compiler_params=pltpu.CompilerParams(
            collective_id=0, has_side_effects=True, vmem_limit_bytes=40 * 1024 * 1024
        ),
        cost_estimate=pl.CostEstimate(
            flops=3_000_000_000, bytes_accessed=2_000_000, transcendentals=1_000_000
        ),
        name="hourglass",
    )(
        in_hbm(tokens.reshape(TOKENS, WIDTH)),
        in_hbm(fine_proj),
        in_hbm(fine_scale),
        in_hbm(jnp.swapaxes(coarse_proj, 1, 2)),
        coarse_scale,
        in_hbm(coarse_cot.reshape(CT, CD)),
    )
    return out_c.reshape(1, CT, CD), out_f.reshape(ROWS, COLS, WIDTH)


def solution(mesh):
    return jax.shard_map(
        body,
        mesh=mesh,
        in_specs=(
            P("row", "col", None),
            P(),
            P(),
            P(None, None, "col"),
            P("col"),
            P("row", None, "col"),
        ),
        out_specs=(P("row", None, "col"), P("row", "col", None)),
        check_vma=False,
    )
```

```python
import contextlib

import jax
import jax.numpy as jnp
from jax import lax
from jax.experimental import pallas as pl
from jax.experimental.pallas import tpu as pltpu
from jax.sharding import PartitionSpec as P

F32 = jnp.float32
BF = jnp.bfloat16
I32 = jnp.int32
EPS = 1e-06
MESH = pl.DeviceIdType.MESH

NY, NZ, NCORE = 2, 8, 2
NR, NC = NY * NZ * NCORE, 16
ROWS, COLS, WIDTH, HEADS = 8, 32, 256, 4
TOKENS = ROWS * COLS
HALO = 320
KEYS = 640
OWN = slice(0, 256)
HALF_HALO = (slice(256, 512), slice(384, 640))
CT = 4 * NC
CD = 64
NM = NY * NCORE

DIRS = ((-1, 0), (1, 0), (0, -1), (0, 1), (-1, -1), (-1, 1), (1, -1), (1, 1))
OPPOSITE = (1, 0, 3, 2, 7, 6, 5, 4)
START = (0, 96, 192, 224, 256, 272, 288, 304)
PLACE = (288, 512, 384, 416, 448, 464, 480, 496)
LENGTH = (96, 96, 32, 32, 16, 16, 16, 16)


def mm(a, b):
    return jnp.dot(a, b, preferred_element_type=F32)


def mt(a, b):
    return lax.dot_general(a, b, (((1,), (1,)), ((), ())), preferred_element_type=F32)


def iota(shape, dim):
    return lax.broadcasted_iota(I32, shape, dim)


def onehot(condition):
    return jnp.where(condition, 1.0, 0.0).astype(BF)


def third(m):
    return (m * 11) >> 5


def edge_parts(p):
    side = p < 64
    m = jnp.where(side, p & 31, p & 15)
    down = third(m)
    across = m - 3 * down
    right = jnp.where(side, (p >> 5) & 1, (p >> 4) & 1)
    bottom = jnp.where(side, 0, ((p - 64) >> 5) & 1)
    used = m < jnp.where(side, 24, 9)
    return side, down, across, right, bottom, used


def kernel(
    tok_hbm, fproj_hbm, fscale_hbm, cproj, cscale, cot_hbm,
    out_c, out_f,
    tok, fproj, fscale, cot, kvx, halo_tok, staging, rq_s, rk_s, iq_s, ik_s, qh, qt, pt, psum, fot, fo_s, kt, fproj_t, wxt, wide, cg, mm_s, inv_s,
    eye_s, w_kv, w_qc, select_s,
    kv, qc, st, ce_s, dp_s, cds_s, dkv, dkv_in, dqo, dqo_in, sb, rb, dyt, ds, dg_halo, rh,
    in_sem, w_sem, halo_ss, halo_rs, cg_ss, cg_rs, kv_ss, kv_rs, qc_ss, qc_rs, st_ss, st_rs,
    dkv_ss, dkv_rs, dqo_ss, dqo_rs, rs_ss, rs_rs, back_ss, back_rs,
):
    row = lax.axis_index("row")
    col = lax.axis_index("col")
    core = row % NCORE
    z = (row // NCORE) % NZ
    y = row // (NCORE * NZ)
    mate = y * NCORE + core
    col_hi = col // 4
    col_lo = col % 4

    def index_of(m, zz):
        return ((m // NCORE) * NZ + zz) * NCORE + m % NCORE

    def neighbour(k):
        return (row + DIRS[k][0] + NR) % NR, (col + DIRS[k][1] + NC) % NC

    z_steps = (4, 3, 5, 2, 6, 1, 7)
    col_steps = sorted(
        ((hi, lo) for hi in range(4) for lo in range(4) if (hi, lo) != (0, 0)),
        key=lambda s: -(2 * min(s[0], 4 - s[0]) + min(s[1], 4 - s[1])),
    )
    z_peers = [(z + d) % NZ for d in z_steps]
    mates = [(mate + d) % NM for d in range(1, NM)]
    col_peers = [((col_hi + hi) % 4) * 4 + (col_lo + lo) % 4 for hi, lo in col_steps]

    open_scope = contextlib.ExitStack()

    def phase(name):
        open_scope.close()
        open_scope.enter_context(jax.named_scope(name))

    barrier = pltpu.get_barrier_semaphore()

    def greet(r, c):
        pl.semaphore_signal(barrier, inc=1, device_id=(r, c), device_id_type=MESH)

    def when_inside(k, action):
        r, c = row + DIRS[k][0], col + DIRS[k][1]

        @pl.when((r >= 0) & (r < NR) & (c >= 0) & (c < NC))
        def _():
            action(k)

    halo_tok[...] = jnp.zeros((KEYS - TOKENS, WIDTH), BF)
    rh[...] = jnp.zeros((HALO, 2 * WIDTH), BF)

    phase("greet")
    for c in col_peers[0:9]:
        greet(row, c)
    for k in range(4, 8):
        greet(*neighbour(k))
    for zz in z_peers[0:3]:
        greet(index_of(mate, zz), col)

    copies = [
        pltpu.make_async_copy(tok_hbm, tok, in_sem.at[0]),
        pltpu.make_async_copy(fproj_hbm, fproj, in_sem.at[1]),
        pltpu.make_async_copy(cot_hbm, cot, in_sem.at[2]),
        pltpu.make_async_copy(fscale_hbm, fscale, in_sem.at[3]),
    ]
    for c in copies:
        c.start()
    weight_copies = [
        pltpu.make_async_copy(cproj.at[s], wxt.at[pl.ds(i * CD, CD)], w_sem.at[i])
        for i, s in enumerate((1, 2, 0))
    ]
    for c in col_peers[9:]:
        greet(row, c)
    for zz in z_peers[3:]:
        greet(index_of(mate, zz), col)
    greet((row + 2 * core - 1 + NR) % NR, col)
    for m in mates:
        greet(index_of(m, z), col)

    phase("inputs_wait")
    def edge_token(slot):
        side, down, across, right, bottom, used = edge_parts(slot)
        return jnp.where(used, (down + 5 * bottom) * COLS + across + (COLS - 3) * right, -1)

    select = onehot(edge_token(iota((128, TOKENS), 0)) == iota((128, TOKENS), 1))
    copies[0].wait()
    token = tok[...]
    staging[...] = mm(select, token).astype(BF)
    phase("barrier_wait")
    pl.semaphore_wait(barrier, len(col_peers) + len(z_peers) + len(mates) + 5)

    def remote(src, dst, ss, rs, r, c):
        return pltpu.make_async_remote_copy(
            src_ref=src, dst_ref=dst, send_sem=ss, recv_sem=rs, device_id=(r, c), device_id_type=MESH
        )

    def halo_copy(k):
        o = OPPOSITE[k]
        if k == 0:
            source = tok.at[pl.ds(0, 96)]
        elif k == 1:
            source = tok.at[pl.ds(TOKENS - 96, 96)]
        else:
            source = staging.at[pl.ds(START[k] - 192, LENGTH[k])]
        target = halo_tok.at[pl.ds(PLACE[o] - TOKENS, LENGTH[o])]
        return remote(source, target, halo_ss.at[k], halo_rs.at[k], *neighbour(k))

    for k in (4, 5, 6, 7, 2, 3, 0, 1):
        when_inside(k, lambda k: halo_copy(k).start())

    phase("own_attend")
    for c in copies[1:4]:
        c.wait()
    for c in weight_copies:
        c.start()
    lane = iota((1, WIDTH), 1)
    head_mask = [jnp.where((lane >> 6) == h, 1.0, 0.0) for h in range(HEADS)]
    blocks = onehot((iota((WIDTH, WIDTH), 0) >> 6) == (iota((WIDTH, WIDTH), 1) >> 6))

    def project(x):
        raw = mm(x, fproj[:, WIDTH : 2 * WIDTH])
        inv = lax.rsqrt(mm((raw * raw).astype(BF), blocks) + EPS)
        return raw, inv, mm(x, fproj[:, 2 * WIDTH :]).astype(BF)

    raw_k, inv_k, value = project(token)
    kvx[OWN, 0:WIDTH] = (raw_k * inv_k).astype(BF)
    kvx[OWN, WIDTH : 2 * WIDTH] = value
    rk_s[...] = raw_k
    ik_s[...] = inv_k
    gain = sum(head_mask[h] * fscale[h] for h in range(HEADS))
    raw_q = mm(token, fproj[:, 0:WIDTH])
    inv_q = lax.rsqrt(mm((raw_q * raw_q).astype(BF), blocks) + EPS)
    unit_q = raw_q * inv_q * gain
    rq_s[...] = raw_q
    iq_s[...] = inv_q

    def head(h, size):
        return slice(h * size, (h + 1) * size)

    half_size = TOKENS // 2
    groups = [(half, pair) for half in range(2) for pair in range(2)]

    def lanes_of(half, pair):
        return head(2 * half + pair, 2 * half_size)

    for half in range(2):
        for h in range(HEADS):
            rows = unit_q[head(half, half_size), :] * head_mask[h]
            qh[head(HEADS * half + h, half_size), :] = rows.astype(BF)
    eye_s[...] = onehot(iota((WIDTH, WIDTH), 0) == iota((WIDTH, WIDTH), 1))

    def transposed(x):
        return mt(eye_s[...], x)

    def spread_heads(ref, x_t):
        for h in range(HEADS):
            rows = head(h, CD)
            for half in range(2):
                lanes = head(HEADS * half + h, half_size)
                ref[rows, lanes] = x_t[rows, head(half, half_size)].astype(BF)

    qt[...] = jnp.zeros((WIDTH, HEADS * TOKENS), BF)
    spread_heads(qt, transposed(unit_q.astype(BF)))

    def near(half, k_row, k_col):
        q = iota((1, 2 * half_size), 1)
        q_row = half * (ROWS // 2) + ((q & (half_size - 1)) >> 5)
        q_col = q & (COLS - 1)
        seen = (jnp.abs(q_row - k_row) <= 3) & (jnp.abs(q_col - k_col) <= 3)
        return jnp.where(seen, 1.0, 0.0)

    def in_image(k_row, k_col, used):
        k_row_all = k_row + row * ROWS
        k_col_all = k_col + col * COLS
        used = used & (k_row_all >= 0) & (k_row_all < ROWS * NR)
        used = used & (k_col_all >= 0) & (k_col_all < COLS * NC)
        return jnp.where(used, k_row, 1000)

    def attend(part, half, values_t, mask):
        keys = kvx[part, 0:WIDTH]
        sums, outs = [], []
        for pair in range(2):
            lanes = lanes_of(half, pair)
            e = jnp.exp(mm(keys, qt[:, lanes])) * mask
            pt[part, lanes] = e
            sums.append(jnp.sum(e, axis=0, keepdims=True))
            outs.append(mm(values_t[head(pair, 2 * CD), :], e.astype(BF)))
        return sums, outs

    values_t = transposed(value).astype(BF)
    n = iota((TOKENS, 1), 0)
    sums = []
    for half in range(2):
        new, outs = attend(OWN, half, values_t, near(half, n >> 5, n & (COLS - 1)))
        sums += new
        for pair in range(2):
            fot[head(2 * half + pair, 2 * CD), :] = outs[pair]

    phase("masks")
    def pooled(r, t):
        return (
            ((r >> 3) == (t >> 7))
            & (((r >> 2) & 1) == ((t >> 2) & 1))
            & ((r & 3) == ((t & 31) >> 3))
        )

    pool = jnp.where(pooled(iota((16, TOKENS), 0), iota((16, TOKENS), 1)), 1.0 / 16.0, 0.0).astype(BF)
    merged_tokens = mm(pool, token)
    n = iota((KEYS - TOKENS, 1), 0)
    side, down, across, right, bottom, used = edge_parts(n - 128)
    k_row = jnp.where(side, down, down - 3 + 11 * bottom)
    k_col = across - 3 + (COLS + 3) * right
    k_row = jnp.where(n < 128, ((n - 32) >> 5) - 3, jnp.where(n < 256, k_row, ((n - 256) >> 5) + ROWS))
    k_col = jnp.where((n >= 128) & (n < 256), k_col, n & (COLS - 1))
    used = (used | (n < 128) | (n >= 256)) & (n >= 32) & (n < 352)
    k_row = in_image(k_row, k_col, used)
    mask_halo = []
    for half in range(2):
        rows = slice(half * 128, half * 128 + 256)
        mask_halo.append(near(half, k_row[rows, :], k_col[rows, :]))

    phase("halo_wait")
    for k in range(8):
        when_inside(k, lambda k: halo_copy(OPPOSITE[k]).wait_recv())

    phase("halo_attend")
    raw_halo, inv_halo, halo_value = project(halo_tok[...])
    kvx[TOKENS:KEYS, 0:WIDTH] = (raw_halo * inv_halo).astype(BF)
    kvx[TOKENS:KEYS, WIDTH : 2 * WIDTH] = halo_value
    halo_t = transposed(halo_value).astype(BF)
    linv, outs_all = [], []
    for half in range(2):
        halo_values = halo_t[:, half * 128 : half * 128 + 256]
        more_sums, more_outs = attend(HALF_HALO[half], half, halo_values, mask_halo[half])
        for pair in range(2):
            g = 2 * half + pair
            linv.append(1.0 / (sums[g] + more_sums[pair]))
            outs_all.append((fot[head(g, 2 * CD), :] + more_outs[pair]) * linv[g])

    def join_heads(pieces):
        rows = []
        for pair in range(2):
            for h in range(2):
                blocks_of = [
                    pieces[2 * half + pair][head(h, CD), head(h, half_size)] for half in range(2)
                ]
                rows.append(jnp.concatenate(blocks_of, axis=1))
        return jnp.concatenate(rows, axis=0)

    fo_t = join_heads(outs_all).astype(BF)

    phase("merge")
    merged = merged_tokens + mt(pool, fo_t)

    def token_sum(x):
        x = x[0:8, :] + x[8:16, :]
        x = jnp.sum(x + pltpu.roll(x, 4, 0), axis=1, keepdims=True)
        return jnp.concatenate([x, x], axis=0)

    inv_m = lax.rsqrt(token_sum(merged * merged) * (1.0 / (4 * WIDTH)) + EPS)

    def part16(i):
        return pl.ds(pl.multiple_of(i * 16, 16), 16)

    cg[part16(col), :] = (merged * inv_m).astype(BF)

    phase("cn_send")
    for c in col_peers:
        remote(cg.at[part16(col)], cg.at[part16(col)], cg_ss, cg_rs, row, c).start()
    col_bytes = pl.ds(0, 16 * len(col_peers))
    cg_all = remote(cg.at[col_bytes], cg.at[col_bytes], cg_ss, cg_rs, row, col_peers[0])

    phase("cn_beside")
    mm_s[...] = merged
    inv_s[...] = inv_m
    depth = iota((CD, 4 * WIDTH), 1)
    wxt[3 * CD : 4 * CD, :] = onehot(depth == col * CD + iota((CD, 4 * WIDTH), 0))
    shift_up = onehot(iota((CD, 2 * CD), 1) == iota((CD, 2 * CD), 0) + CD)
    cot_high = mm(cot[...], shift_up)
    low_lane = iota((1, 2 * CD), 1) < CD
    for c in weight_copies:
        c.wait()
    for ab in range(4):
        wide[head(ab, WIDTH), :] = mt(eye_s[...], wxt[:, head(ab, WIDTH)]).astype(BF)
    for half, pair in groups:
        lanes = lanes_of(half, pair)
        for part in (OWN, HALF_HALO[half]):
            pt[part, lanes] = pt[part, lanes] * linv[2 * half + pair]
    for k in range(8):
        when_inside(k, lambda k: halo_copy(k).wait_send())
    phase("cn_wait")
    cg_all.wait_recv()

    phase("coarse_projection")
    part_of = (iota((16 * NC, 1), 0) >> 2) & 3
    part_mask = [jnp.where(part_of == ab, 1.0, 0.0) for ab in range(4)]
    upper_rows = iota((1, 8, 1), 1) < 4

    def by_part(x):
        return jnp.concatenate([(x * part_mask[ab]).astype(BF) for ab in range(4)], axis=1)

    made = mm(by_part(cg[...].astype(F32)), wide[...]).reshape(NC, 2, 8, 4 * CD)
    made = made[:, 0] + made[:, 1]
    made = made + pltpu.roll(made, 4, 1)
    made = made.reshape(NC // 2, 2, 8, 4 * CD)
    made = jnp.where(upper_rows, made[:, 0], made[:, 1]).reshape(CT, 4 * CD)
    made_kv = made[:, 0 : 2 * CD]
    made_qo = made[:, 2 * CD : 4 * CD]

    def low_sum(x):
        return jnp.sum(jnp.where(low_lane, x, 0.0), axis=1, keepdims=True)

    coarse_gain = cscale[0]
    inv_ck = lax.rsqrt(low_sum(made_kv * made_kv) + EPS)
    inv_cq = lax.rsqrt(low_sum(made_qo * made_qo) + EPS)
    own_kv = jnp.where(low_lane, made_kv * inv_ck, made_kv)
    own_qc = jnp.where(low_lane, made_qo * inv_cq * coarse_gain, cot_high)

    def block(i):
        return pl.ds(pl.multiple_of(i * CT, CT), CT)

    kv[block(z), :] = own_kv.astype(BF)
    qc[block(mate), :] = own_qc.astype(BF)

    phase("kv_send")
    def kv_copy(slot_of, to, d):
        return remote(
            kv.at[block(slot_of)], kv.at[block(slot_of)], kv_ss, kv_rs.at[d], index_of(mate, to), col
        )

    for d, zz in zip(z_steps, z_peers):
        kv_copy(z, zz, d).start()
    for m in mates:
        remote(qc.at[block(mate)], qc.at[block(mate)], qc_ss, qc_rs, index_of(m, z), col).start()
    z_bytes = pl.ds(0, CT * len(z_peers))
    m_bytes = pl.ds(0, CT * len(mates))
    to_z = (index_of(mate, z_peers[0]), col)
    to_mate = (index_of(mates[0], z), col)
    qc_all = remote(qc.at[m_bytes], qc.at[m_bytes], qc_ss, qc_rs, *to_mate)
    phase("kv_beside")
    cg_all.wait_send()
    for ab in range(4):
        w_kv[head(ab, 2 * CD), :] = wxt[0 : 2 * CD, head(ab, WIDTH)]
        w_qc[head(ab, 2 * CD), :] = wxt[2 * CD : 4 * CD, head(ab, WIDTH)]
    fo_s[...] = fo_t.astype(F32)
    kt[...] = transposed(kvx[:, 0:WIDTH]).astype(BF)
    for i in range(3):
        fproj_t[head(i, WIDTH), :] = transposed(fproj[:, head(i, WIDTH)]).astype(BF)
    phase("qc_wait")
    qc_all.wait_recv()
    queries = qc[...].astype(F32)
    q_low = jnp.where(low_lane, queries, 0.0).astype(BF)
    cot_only = jnp.where(low_lane, 0.0, queries).astype(BF)
    eye_small = eye_s[0 : 2 * CD, 0 : 2 * CD]
    q_low_t = mt(eye_small, q_low).astype(BF)
    cot_t = mt(eye_small, cot_only).astype(BF)

    phase("kv_scores")
    c_sum = jnp.zeros((1, NM * CT), F32)
    c_weighted = jnp.zeros((1, NM * CT), F32)
    for steps in ((0, 1, 7), (2, 6), (3, 5, 4)):
        sources = [(z + NZ - d) % NZ for d in steps]
        for d, source in zip(steps, sources):
            if d:
                kv_copy(source, source, d).wait_recv()
        some = jnp.concatenate([kv[block(source), :] for source in sources], axis=0)
        e = jnp.exp(mm(some, q_low_t))
        p = mm(some, cot_t)
        for i, source in enumerate(sources):
            ce_s[block(source), :] = e[head(i, CT), :]
            dp_s[block(source), :] = p[head(i, CT), :]
        c_sum = c_sum + jnp.sum(e, axis=0, keepdims=True)
        c_weighted = c_weighted + jnp.sum(e * p, axis=0, keepdims=True)
    phase("stats_send")
    st[mate, 0:1, :] = c_sum
    st[mate, 1:2, :] = c_weighted
    for m in mates:
        remote(st.at[mate], st.at[mate], st_ss, st_rs, index_of(m, z), col).start()
    st_bytes = pl.ds(0, len(mates))
    st_all = remote(st.at[st_bytes], st.at[st_bytes], st_ss, st_rs, *to_mate)
    phase("stats_beside")
    kv_t = mt(eye_s[0 : 2 * CD, 0 : 2 * CD], kv[...]).astype(BF)
    o_t = mm(kv_t, ce_s[...].astype(BF))
    remote(kv.at[z_bytes], kv.at[z_bytes], kv_ss, kv_rs.at[1], *to_z).wait_send()
    qc_all.wait_send()
    phase("stats_wait")
    st_all.wait_recv()
    phase("dkv_make")
    totals = (st[0] + st[1]) + (st[2] + st[3])
    c_inv = 1.0 / totals[0:1, :]
    c_delta = totals[1:2, :] * c_inv
    both = jnp.concatenate([q_low, cot_only], axis=0)
    for targets in (z_peers[0:3], z_peers[3:5], z_peers[5:7] + [z]):
        cp = jnp.concatenate([ce_s[block(zz), :] for zz in targets], axis=0) * c_inv
        cds = cp * (jnp.concatenate([dp_s[block(zz), :] for zz in targets], axis=0) - c_delta)
        cds = cds.astype(BF)
        made_here = mm(jnp.concatenate([cds, cp.astype(BF)], axis=1), both).astype(BF)
        for i, zz in enumerate(targets):
            cds_s[block(zz), :] = cds[head(i, CT), :]
            dkv[block(zz), :] = made_here[head(i, CT), :]
            if zz is not z:
                remote(
                    dkv.at[block(zz)], dkv_in.at[block(z)], dkv_ss, dkv_rs, index_of(mate, zz), col
                ).start()
    dkv_all = remote(dkv.at[z_bytes], dkv_in.at[z_bytes], dkv_ss, dkv_rs, *to_z)
    phase("dq_make")
    dq_t = mm(kv_t, cds_s[...])
    dqo_t = jnp.where(iota((2 * CD, 1), 0) < CD, dq_t, o_t * c_inv).astype(BF)
    dqo[...] = transposed(dqo_t).astype(BF)
    for m in mates:
        remote(dqo.at[block(m)], dqo_in.at[block(mate)], dqo_ss, dqo_rs, index_of(m, z), col).start()
    dqo_all = remote(dqo.at[m_bytes], dqo_in.at[m_bytes], dqo_ss, dqo_rs, *to_mate)
    dkv_in[block(z), :] = dkv[block(z), :]
    dqo_in[block(mate), :] = dqo[block(mate), :]
    st_all.wait_send()
    phase("dqo_wait")
    dqo_all.wait_recv()
    phase("dq_unit")
    d_qo = dqo_in[head(0, CT), :].astype(F32)
    for m in range(1, NM):
        d_qo = d_qo + dqo_in[head(m, CT), :].astype(F32)
    g_q = (coarse_gain * inv_cq) * (d_qo - made_qo * (inv_cq * inv_cq * low_sum(d_qo * made_qo)))

    def repeated(g):
        g = g.reshape(NC // 2, 8, 2 * CD)
        turned = pltpu.roll(g, 4, 1)
        pair = [jnp.where(upper_rows, g, turned), jnp.where(upper_rows, turned, g)]
        g = jnp.stack(pair, axis=1).reshape(NC, 1, 8, 2 * CD)
        return jnp.broadcast_to(g, (NC, 2, 8, 2 * CD)).reshape(16 * NC, 2 * CD)

    term_qc = mm(by_part(repeated(jnp.where(low_lane, g_q, cot_high))), w_qc[...])
    phase("dkv_wait")
    dkv_all.wait_recv()
    phase("term")
    d_kv = dkv_in[head(0, CT), :].astype(F32)
    for i in range(1, NZ):
        d_kv = d_kv + dkv_in[head(i, CT), :].astype(F32)
    g_k = inv_ck * (d_kv - made_kv * (inv_ck * inv_ck * low_sum(d_kv * made_kv)))
    g_kv = jnp.where(low_lane, g_k, d_kv)

    sb[...] = (term_qc + mm(by_part(repeated(g_kv)), w_kv[...])).astype(BF)
    phase("rs_send")
    for c in col_peers:
        remote(sb.at[part16(c)], rb.at[part16(col)], rs_ss, rs_rs, row, c).start()
    rs_all = remote(sb.at[col_bytes], rb.at[col_bytes], rs_ss, rs_rs, row, col_peers[0])
    phase("rs_beside")
    rb[part16(col), :] = sb[part16(col), :]
    out_c[...] = pltpu.roll(made_qo + d_qo, CD, 1)[:, 0:CD]
    dkv_all.wait_send()
    dqo_all.wait_send()
    select_s[...] = onehot(edge_token(iota((TOKENS, 128), 1)) == iota((TOKENS, 128), 0))
    spread = onehot(pooled(iota((TOKENS, 16), 1), iota((TOKENS, 16), 0)))
    dyt[...] = jnp.zeros((WIDTH, HEADS * TOKENS), BF)
    spread_t = onehot(pooled(iota((16, TOKENS), 0), iota((16, TOKENS), 1)))
    lane = iota((CD, HEADS * TOKENS), 1)
    entry = iota((CD, HEADS * TOKENS), 0)
    query = (lane >> 9) * half_size + (lane & (half_size - 1))
    collect = onehot((((lane >> 7) & 3) == (entry >> 4)) & pooled(entry & 15, query))
    sums = []
    for half in range(2):
        lanes = head(half, HEADS * half_size)
        total = [mt(pt[part, lanes].astype(BF), collect[:, lanes]) for part in (OWN, HALF_HALO[half])]
        sums.append(total)
    zeros = jnp.zeros((128, CD), F32)
    halo_sum = jnp.concatenate([sums[0][1], zeros], axis=0) + jnp.concatenate([zeros, sums[1][1]], axis=0)
    share_sum = jnp.concatenate([sums[0][0] + sums[1][0], halo_sum], axis=0)
    high = share_sum.astype(BF)
    low = (share_sum - high.astype(F32)).astype(BF)
    psum[:, 0:CD] = high
    psum[:, CD : 2 * CD] = low
    phase("rs_wait")
    rs_all.wait_recv()
    phase("norm_back")
    grad = rb[0:16, :].astype(F32)
    for c in range(1, NC):
        grad = grad + rb[head(c, 16), :].astype(F32)

    merged = mm_s[...]
    inv_m = inv_s[...]
    grad = inv_m * (grad - merged * (inv_m * inv_m * token_sum(grad * merged) * (1.0 / (4 * WIDTH))))
    dy_blocks = (grad * (1.0 / 16.0)).astype(BF)
    dy_t = mm(mt(eye_s[...], dy_blocks).astype(BF), spread_t)
    dy = mm(spread, dy_blocks)
    by_block = jnp.concatenate([dy_blocks.astype(F32) * head_mask[h] for h in range(HEADS)], axis=0).astype(BF)
    by_block = jnp.concatenate([by_block, by_block], axis=0)

    phase("halo_back")
    spread_heads(dyt, dy_t)
    product = dy_t * fo_s[...]
    by_head = [jnp.sum(product[head(h, CD), :], axis=0, keepdims=True) for h in range(HEADS)]
    delta = [
        jnp.concatenate([by_head[2 * pair + h][:, head(half, half_size)] for h in range(2)], axis=1)
        for half, pair in groups
    ]

    def score_side(part, half):
        values = kvx[part, WIDTH : 2 * WIDTH]
        for pair in range(2):
            lanes = lanes_of(half, pair)
            d_p = mm(values, dyt[:, lanes]) - delta[2 * half + pair]
            ds[part, lanes] = (pt[part, lanes] * d_p).astype(BF)

    d_v = mm(psum[...], by_block)
    dg_halo[0:96, WIDTH : 2 * WIDTH] = d_v[288:384, :].astype(BF)
    dg_halo[96:192, WIDTH : 2 * WIDTH] = d_v[512:608, :].astype(BF)
    dg_halo[192:320, WIDTH : 2 * WIDTH] = d_v[384:512, :].astype(BF)

    def back_copy(k):
        o = OPPOSITE[k]
        source = dg_halo.at[pl.ds(START[k], LENGTH[k])]
        target = rh.at[pl.ds(START[o], LENGTH[o])]
        return remote(source, target, back_ss.at[k], back_rs.at[k], *neighbour(k))

    upper = slice(0, HEADS * half_size)
    lower = slice(HEADS * half_size, 2 * HEADS * half_size)
    score_side(HALF_HALO[0], 0)
    d_k_upper = mm(ds[HALF_HALO[0], upper], qh[upper, :])
    score_side(HALF_HALO[1], 1)
    d_k_lower = mm(ds[HALF_HALO[1], lower], qh[lower, :])
    dg_halo[192:320, 0:WIDTH] = (d_k_upper[128:256, :] + d_k_lower[0:128, :]).astype(BF)
    for k in (4, 5, 6, 7, 2, 3):
        when_inside(k, lambda k: back_copy(k).start())
    dg_halo[0:96, 0:WIDTH] = d_k_upper[32:128, :].astype(BF)
    when_inside(0, lambda k: back_copy(k).start())
    dg_halo[96:192, 0:WIDTH] = d_k_lower[128:224, :].astype(BF)
    when_inside(1, lambda k: back_copy(k).start())

    phase("own_back")
    score_side(OWN, 0)
    score_side(OWN, 1)
    d_k = mm(ds[OWN, :], qh[...])
    d_v = d_v[OWN, :]
    phase("query_back")
    pieces = []
    for half, pair in groups:
        lanes = lanes_of(half, pair)
        from_own = mm(kt[head(pair, 2 * CD), OWN], ds[OWN, lanes])
        from_halo = mm(kt[head(pair, 2 * CD), HALF_HALO[half]], ds[HALF_HALO[half], lanes])
        pieces.append(from_own + from_halo)
    d_q = transposed(join_heads(pieces).astype(BF))
    raw_q = rq_s[...]
    inv_q = iq_s[...]
    g_q = gain * inv_q * (d_q - raw_q * (inv_q * inv_q * mm((d_q * raw_q).astype(BF), blocks)))
    result = dy + mm(g_q.astype(BF), fproj_t[0:WIDTH, :])
    rs_all.wait_send()

    phase("back_wait")
    for k in range(8):
        when_inside(k, lambda k: back_copy(OPPOSITE[k]).wait_recv())
    phase("finish")
    received = mm(select_s[...], rh[192:320, :]) + jnp.concatenate(
        [
            rh[0:96, :].astype(F32),
            jnp.zeros((TOKENS - 192, 2 * WIDTH), F32),
            rh[96:192, :].astype(F32),
        ],
        axis=0,
    )
    d_k = d_k + received[:, 0:WIDTH]
    d_v = d_v + received[:, WIDTH : 2 * WIDTH]
    raw_k = rk_s[...]
    inv_k = ik_s[...]
    g_k = inv_k * (d_k - raw_k * (inv_k * inv_k * mm((d_k * raw_k).astype(BF), blocks)))
    g_kv = jnp.concatenate([g_k.astype(BF), d_v.astype(BF)], axis=1)
    result = result + mm(g_kv, fproj_t[WIDTH:, :])
    out_f[...] = result.astype(BF)
    for k in range(8):
        when_inside(k, lambda k: back_copy(k).wait_send())
    open_scope.close()


def in_hbm(x):
    return pltpu.with_memory_space_constraint(x, pltpu.HBM)


def body(tokens, fine_proj, fine_scale, coarse_proj, coarse_scale, coarse_cot):
    vmem = pl.BlockSpec(memory_space=pltpu.VMEM)
    smem = pl.BlockSpec(memory_space=pltpu.SMEM)
    hbm = pl.BlockSpec(memory_space=pltpu.HBM)
    dma = pltpu.SemaphoreType.DMA
    out_c, out_f = pl.pallas_call(
        kernel,
        out_shape=(
            jax.ShapeDtypeStruct((CT, CD), F32),
            jax.ShapeDtypeStruct((TOKENS, WIDTH), BF),
        ),
        in_specs=[hbm, hbm, hbm, hbm, smem, hbm],
        out_specs=(vmem, vmem),
        scratch_shapes=[
            pltpu.VMEM((TOKENS, WIDTH), BF),
            pltpu.VMEM((WIDTH, 3 * WIDTH), BF),
            pltpu.SMEM((HEADS,), F32),
            pltpu.VMEM((CT, CD), BF),
            pltpu.VMEM((KEYS, 2 * WIDTH), BF),
            pltpu.VMEM((KEYS - TOKENS, WIDTH), BF),
            pltpu.VMEM((128, WIDTH), BF),
            pltpu.VMEM((TOKENS, WIDTH), F32),
            pltpu.VMEM((TOKENS, WIDTH), F32),
            pltpu.VMEM((TOKENS, WIDTH), F32),
            pltpu.VMEM((TOKENS, WIDTH), F32),
            pltpu.VMEM((HEADS * TOKENS, WIDTH), BF),
            pltpu.VMEM((WIDTH, HEADS * TOKENS), BF),
            pltpu.VMEM((KEYS, HEADS * TOKENS), F32),
            pltpu.VMEM((KEYS, 2 * CD), BF),
            pltpu.VMEM((2 * WIDTH, TOKENS), F32),
            pltpu.VMEM((TOKENS, WIDTH), F32),
            pltpu.VMEM((WIDTH, KEYS), BF),
            pltpu.VMEM((3 * WIDTH, WIDTH), BF),
            pltpu.VMEM((4 * CD, 4 * WIDTH), BF),
            pltpu.VMEM((4 * WIDTH, 4 * CD), BF),
            pltpu.VMEM((16 * NC, WIDTH), BF),
            pltpu.VMEM((16, WIDTH), F32),
            pltpu.VMEM((16, 1), F32),
            pltpu.VMEM((WIDTH, WIDTH), BF),
            pltpu.VMEM((8 * CD, WIDTH), BF),
            pltpu.VMEM((8 * CD, WIDTH), BF),
            pltpu.VMEM((TOKENS, 128), BF),
            pltpu.VMEM((NZ * CT, 2 * CD), BF),
            pltpu.VMEM((NM * CT, 2 * CD), BF),
            pltpu.VMEM((NM, 2, NM * CT), F32),
            pltpu.VMEM((NZ * CT, NM * CT), F32),
            pltpu.VMEM((NZ * CT, NM * CT), F32),
            pltpu.VMEM((NZ * CT, NM * CT), BF),
            pltpu.VMEM((NZ * CT, 2 * CD), BF),
            pltpu.VMEM((NZ * CT, 2 * CD), BF),
            pltpu.VMEM((NM * CT, 2 * CD), BF),
            pltpu.VMEM((NM * CT, 2 * CD), BF),
            pltpu.VMEM((16 * NC, WIDTH), BF),
            pltpu.VMEM((16 * NC, WIDTH), BF),
            pltpu.VMEM((WIDTH, HEADS * TOKENS), BF),
            pltpu.VMEM((KEYS, HEADS * TOKENS), BF),
            pltpu.VMEM((HALO, 2 * WIDTH), BF),
            pltpu.VMEM((HALO, 2 * WIDTH), BF),
            dma((4,)), dma((3,)), dma((8,)), dma((8,)),
            dma(()), dma(()), dma(()), dma((NZ,)), dma(()), dma(()), dma(()), dma(()),
            dma(()), dma(()), dma(()), dma(()), dma(()), dma(()),
            dma((8,)), dma((8,)),
        ],
        compiler_params=pltpu.CompilerParams(
            collective_id=0, has_side_effects=True, vmem_limit_bytes=40 * 1024 * 1024
        ),
        cost_estimate=pl.CostEstimate(
            flops=3_000_000_000, bytes_accessed=2_000_000, transcendentals=1_000_000
        ),
        name="hourglass",
    )(
        in_hbm(tokens.reshape(TOKENS, WIDTH)),
        in_hbm(fine_proj),
        in_hbm(fine_scale),
        in_hbm(jnp.swapaxes(coarse_proj, 1, 2)),
        coarse_scale,
        in_hbm(coarse_cot.reshape(CT, CD)),
    )
    return out_c.reshape(1, CT, CD), out_f.reshape(ROWS, COLS, WIDTH)


def solution(mesh):
    return jax.shard_map(
        body,
        mesh=mesh,
        in_specs=(
            P("row", "col", None),
            P(),
            P(),
            P(None, None, "col"),
            P("col"),
            P("row", None, "col"),
        ),
        out_specs=(P("row", None, "col"), P("row", "col", None)),
        check_vma=False,
    )
```
